512 devices in a mesh: batch: 16 (over x, z_hi, core), head: 32 (over z_lo, y).
Axes of the slice: x: 4, y: 4, z: 16 (z_hi: 2, z_lo: 8; z = z_hi * 8 + z_lo), core: 2. Of those that a mesh axis runs over, the one named last changes fastest.
Arguments:
- student_patches: bfloat16 [64, 256, 256], P('batch')
- teacher_patches: bfloat16 [64, 256, 256], P('batch')
- mask_index: int32 [64, 128], P('batch'), may hold values from 0 to 255, as said below
- weight: bfloat16 [256, 65536], P(None, 'head')
Outputs:
- grad_rows: float32 [64, 128, 256], P('batch')
- grad_weight: float32 [256, 65536], P('batch', 'head')
- loss: float32 [], replicated
The draws below stay inside these ranges and needn't reach their ends.
Inputs may be any that keep to these rules, and one draw needn't show every extreme that they name: `mask_index`: the 128 positions of one crop are distinct.
All inputs are finite; a program needn't handle non-finite values.
Results may differ from the reference program's by a relative error of at most 0.003.
Values sent between devices are 32-bit elements; how exact they have to be, the bound alone decides.
No kernel may reach another device: no remote copies, remote signals or barrier semaphores. Data moves between devices by JAX's collectives and lax.ppermute only.
A program may use at most 64 MiB of HBM per device.

```python
import math
import jax
import jax.numpy as jnp
from jax import lax

BOT = 256
K = 65536
PATCH = 256
MASKED = 128
VIEWS = 64


def shared_parts(key):
    first_key, second_key, third_key, fourth_key = jax.random.split(key, 4)
    protos = jax.random.normal(first_key, (BOT, K), jnp.float32) / 16.0
    picked = jax.random.randint(second_key, (VIEWS, PATCH), 0, K)
    centers = jax.random.normal(third_key, (2, BOT), jnp.float32) / 16.0
    crop_major = jax.random.bernoulli(fourth_key, 0.8, (VIEWS, 1, 1))
    return (protos, picked, centers, crop_major)


def mixed_from(key, inner_key, center_coef, mix_low, mix_high, scale_top):
    protos, picked, centers, crop_major = shared_parts(key)
    first_key, second_key, third_key = jax.random.split(inner_key, 3)
    columns = jnp.moveaxis(protos[:, picked], 0, -1)
    crop_center = jnp.where(crop_major, centers[0][None, None, :], centers[1][None, None, :])
    noise = jax.random.normal(first_key, (VIEWS, PATCH, BOT), jnp.float32) / 16.0
    mixing = jax.random.uniform(second_key, (VIEWS, PATCH, 1), jnp.float32, mix_low, mix_high)
    scales = jnp.exp(jax.random.uniform(third_key, (VIEWS, PATCH, 1), jnp.float32, 0.0, math.log(scale_top)))
    rows = center_coef * crop_center + mixing * columns + (1.0 - mixing) * noise
    return (rows * scales).astype(jnp.bfloat16)


def draw_student_patches(key, part):
    inner_key = jax.random.fold_in(key, 11)
    return mixed_from(key, inner_key, 0.6, 0.3, 0.8, 4.0)


def draw_teacher_patches(key, part):
    inner_key = jax.random.fold_in(key, 13)
    return mixed_from(key, inner_key, 0.6, 0.3, 0.8, 4.0)


def weight_from(key, inner_key, center_coef, scale_low, scale_high):
    protos, picked, centers, crop_major = shared_parts(key)
    label_key, scale_key = jax.random.split(inner_key)
    col_minor = jax.random.bernoulli(label_key, 0.2, (1, K))
    col_center = jnp.where(col_minor, centers[0][:, None], centers[1][:, None])
    scales = jnp.exp(jax.random.uniform(scale_key, (1, K), jnp.float32, math.log(scale_low), math.log(scale_high)))
    return ((center_coef * col_center + protos) * scales).astype(jnp.bfloat16)


def draw_weight(key, part):
    inner_key = jax.random.fold_in(key, 17)
    return weight_from(key, inner_key, 0.6, 0.5, 2.0)


def draw_mask_index(key, part):
    inner_key = jax.random.fold_in(key, 19)
    view_keys = jax.random.split(inner_key, VIEWS)

    def one_view(view_key):
        return jax.random.permutation(view_key, PATCH)[:MASKED]
    return jax.vmap(one_view)(view_keys).astype(jnp.int32)


def setup_inputs(seed: int = 0) -> dict:
    seeds = jax.random.split(jax.random.key(seed), 5)
    return {
        "student_patches": draw_student_patches(jax.random.fold_in(seeds[4], 71), 0),
        "teacher_patches": draw_teacher_patches(jax.random.fold_in(seeds[4], 71), 0),
        "mask_index": draw_mask_index(jax.random.fold_in(seeds[4], 71), 0),
        "weight": draw_weight(jax.random.fold_in(seeds[4], 71), 0),
    }


TEACHER_TEMP = 0.07
STUDENT_TEMP = 0.1
EPSILON = 1e-06
HIGH = lax.Precision.HIGHEST

def unit_rows(values):
    floats = values.astype(jnp.float32)
    inverse = lax.rsqrt(lax.optimization_barrier(jnp.sum(floats * floats, axis=-1, keepdims=True)) + EPSILON)
    return (floats * inverse, inverse)

def reference(student_patches, teacher_patches, mask_index, weight):
    feature_dim = weight.shape[0]
    gather_index = mask_index[:, :, None].astype(jnp.int32)
    student_rows = jnp.take_along_axis(student_patches, gather_index, axis=1).reshape(-1, feature_dim)
    teacher_rows = jnp.take_along_axis(teacher_patches, gather_index, axis=1).reshape(-1, feature_dim)
    student_unit, student_inv = unit_rows(student_rows)
    teacher_unit, teacher_inv = unit_rows(teacher_rows)
    student_norm = student_unit.astype(jnp.bfloat16)
    teacher_norm = teacher_unit.astype(jnp.bfloat16)
    wfloat = weight.astype(jnp.float32)
    weight_inv = lax.rsqrt(lax.optimization_barrier(jnp.sum(wfloat * wfloat, axis=0, keepdims=True)) + EPSILON)
    weight_unit = wfloat * weight_inv
    weight_norm = weight_unit.astype(jnp.bfloat16)
    total_rows = student_rows.shape[0]
    block = min(512, total_rows)
    blocks = total_rows // block
    teacher_blocks = teacher_norm.reshape(blocks, block, feature_dim)
    student_blocks = student_norm.reshape(blocks, block, feature_dim)

    def teacher_exp(tblock):
        return jnp.exp(jnp.dot(tblock, weight_norm, preferred_element_type=jnp.float32) / TEACHER_TEMP)

    def first_pass(carry, tblock):
        expo = teacher_exp(tblock)
        return (carry + lax.optimization_barrier(jnp.sum(expo, axis=0)), None)
    col_total, _ = lax.scan(first_pass, jnp.zeros((weight.shape[1],), jnp.float32), teacher_blocks)
    col_scale = 1.0 / col_total
    for sweep in range(2):

        def sweep_pass(carry, tblock):
            expo = teacher_exp(tblock)
            row_scale = 1.0 / jnp.dot(expo, col_scale, precision=HIGH)
            return (carry + jnp.dot(row_scale, expo, precision=HIGH), None)
        col_total, _ = lax.scan(sweep_pass, jnp.zeros((weight.shape[1],), jnp.float32), teacher_blocks)
        col_scale = 1.0 / col_total

    def final_pass(carry, pair):
        tblock, sblock = pair
        expo = teacher_exp(tblock)
        row_scale = 1.0 / jnp.dot(expo, col_scale, precision=HIGH)
        targets = row_scale[:, None] * expo * col_scale[None, :]
        logits = jnp.dot(sblock, weight_norm, preferred_element_type=jnp.float32)
        student_exp = jnp.exp(logits / STUDENT_TEMP)
        partition = lax.optimization_barrier(jnp.sum(student_exp, axis=1))
        row_loss = jnp.log(partition) - lax.optimization_barrier(jnp.sum(targets * logits, axis=1)) / STUDENT_TEMP
        grad_logits = ((student_exp / partition[:, None] - targets) / STUDENT_TEMP).astype(jnp.bfloat16)
        grad_student = jnp.dot(grad_logits, weight_norm.T, preferred_element_type=jnp.float32)
        grad_unit = carry[0] + jnp.dot(sblock.T, grad_logits, preferred_element_type=jnp.float32)
        return ((grad_unit, carry[1] + jnp.sum(row_loss)), grad_student)
    start = (jnp.zeros(weight.shape, jnp.float32), jnp.zeros((), jnp.float32))
    (grad_unit, loss_sum), grad_student = lax.scan(final_pass, start, (teacher_blocks, student_blocks))
    grad_student = grad_student.reshape(total_rows, feature_dim)
    inner = lax.optimization_barrier(jnp.sum(student_unit * grad_student, axis=1, keepdims=True))
    grad_rows = (student_inv * (grad_student - student_unit * inner)).reshape(mask_index.shape[0], mask_index.shape[1], feature_dim)
    col_inner = lax.optimization_barrier(jnp.sum(weight_unit * grad_unit, axis=0, keepdims=True))
    grad_weight = weight_inv * (grad_unit - weight_unit * col_inner)
    return (grad_rows, grad_weight, loss_sum / total_rows)
```

```python
import jax
import jax.numpy as jnp
from jax import lax
from jax.sharding import PartitionSpec as P

TEACHER_TEMP = 0.07
STUDENT_TEMP = 0.1
EPSILON = 1e-06


def unit_rows(values):
    inverse = lax.rsqrt(jnp.sum(values * values, axis=-1, keepdims=True) + EPSILON)
    return (values * inverse, inverse)


def contract_rows(left, right):
    return lax.dot_general(
        left, right, (((0,), (0,)), ((), ())), preferred_element_type=jnp.float32
    )


def pick_rows(patches, onehot):
    rows = lax.dot_general(
        onehot, patches, (((2,), (1,)), ((0,), (0,))), preferred_element_type=jnp.float32
    )
    return rows.reshape(-1, patches.shape[-1])


def share_all(block, axis, groups=None, count=None):
    copies = jnp.broadcast_to(block[None], (count,) + block.shape)
    return lax.all_to_all(copies, axis, 0, 0, axis_index_groups=groups)


def sum_small(vector, axis):
    count = lax.axis_size(axis)
    return jnp.sum(share_all(vector.reshape(-1, 128), axis, None, count), axis=0).reshape(
        vector.shape
    )


def scatter_sum(blocks, axis, groups):
    return jnp.sum(lax.all_to_all(blocks, axis, 0, 0, axis_index_groups=groups), axis=0)


def per_device(student_patches, teacher_patches, mask_index, weight):
    view_count, masked_count = mask_index.shape
    feature_dim, columns = weight.shape
    batch_index = lax.axis_index("batch")
    head_index = lax.axis_index("head")
    x_groups = [[4 * x + rest for x in range(4)] for rest in range(4)]
    y_groups = [[4 * z + y for y in range(4)] for z in range(8)]
    z_groups = [[4 * z + y for z in range(8)] for y in range(4)]
    core = batch_index % 2
    z_high = (batch_index // 2) % 2

    patch = lax.broadcasted_iota(jnp.int32, mask_index.shape + (student_patches.shape[1],), 2)
    onehot = (mask_index[:, :, None] == patch).astype(jnp.bfloat16)
    student_unit, student_inv = unit_rows(pick_rows(student_patches, onehot))
    teacher_unit, _ = unit_rows(pick_rows(teacher_patches, onehot))
    student_norm = student_unit.astype(jnp.bfloat16)
    teacher_norm = teacher_unit.astype(jnp.bfloat16)
    wfloat = weight.astype(jnp.float32)
    weight_inv = lax.rsqrt(jnp.sum(wfloat * wfloat, axis=0, keepdims=True) + EPSILON)
    weight_unit = wfloat * weight_inv
    weight_norm = weight_unit.astype(jnp.bfloat16)
    teacher_exp = jnp.exp(
        jnp.dot(teacher_norm, weight_norm, preferred_element_type=jnp.float32) / TEACHER_TEMP
    )
    col_scale = 1.0 / sum_small(jnp.sum(teacher_exp, axis=0), "batch")
    for _ in range(2):
        row_scale = 1.0 / sum_small(jnp.sum(teacher_exp * col_scale[None, :], axis=1), "head")
        col_scale = 1.0 / sum_small(jnp.sum(teacher_exp * row_scale[:, None], axis=0), "batch")
    student_logits = jnp.dot(student_norm, weight_norm, preferred_element_type=jnp.float32)
    student_exp = jnp.exp(student_logits / STUDENT_TEMP)
    partition_part = jnp.sum(student_exp, axis=1)
    scaled = teacher_exp * col_scale[None, :]
    row_part = jnp.sum(scaled, axis=1)
    weighted_part = jnp.sum(scaled * student_logits, axis=1)
    row_total, partition, weighted = sum_small(
        jnp.stack([row_part, partition_part, weighted_part]), "head"
    )
    row_scale = 1.0 / row_total
    row_loss = jnp.log(partition) - row_scale * weighted / STUDENT_TEMP
    total_rows = row_loss.shape[0] * lax.axis_size("batch")
    loss_part = jnp.broadcast_to(jnp.sum(row_loss), (1, 128))
    loss = sum_small(loss_part, "batch")[0, 0] / total_rows

    targets = row_scale[:, None] * scaled
    grad_logits = ((student_exp / partition[:, None] - targets) / STUDENT_TEMP).astype(jnp.bfloat16)

    grad_unit = contract_rows(student_norm, grad_logits)
    col_inner = jnp.sum(weight_unit * grad_unit, axis=0, keepdims=True)
    grad_full = weight_inv * (grad_unit - weight_unit * col_inner)
    parts = grad_full.reshape(4, 2, 2, feature_dim // 16, columns)
    keep = lax.dynamic_index_in_dim(parts, core, 2, keepdims=False)
    send = lax.dynamic_index_in_dim(parts, 1 - core, 2, keepdims=False)
    parts = keep + lax.ppermute(send, "batch", [(i, i ^ 1) for i in range(16)])
    parts = scatter_sum(parts, "batch", x_groups)
    keep = lax.dynamic_index_in_dim(parts, z_high, 0, keepdims=False)
    send = lax.dynamic_index_in_dim(parts, 1 - z_high, 0, keepdims=False)
    grad_weight = keep + lax.ppermute(send, "batch", [(i, i ^ 2) for i in range(16)])

    grad_local = lax.dot_general(
        grad_logits, weight_norm, (((1,), (1,)), ((), ())), preferred_element_type=jnp.float32
    )
    total = grad_local.shape[0]
    piece = scatter_sum(grad_local.reshape(4, total // 4, feature_dim), "head", y_groups)
    piece = scatter_sum(piece.reshape(8, total // 32, feature_dim), "head", z_groups)
    first = (head_index % 4) * (total // 4) + (head_index // 4) * (total // 32)
    unit_piece = lax.dynamic_slice_in_dim(student_unit, first, total // 32, 0)
    inv_piece = lax.dynamic_slice_in_dim(student_inv, first, total // 32, 0)
    inner = jnp.sum(unit_piece * piece, axis=1, keepdims=True)
    piece = inv_piece * (piece - unit_piece * inner)
    piece = share_all(piece, "head", z_groups, 8).reshape(total // 4, feature_dim)
    grad_rows = share_all(piece, "head", y_groups, 4).reshape(
        view_count, masked_count, feature_dim
    )
    return (grad_rows, grad_weight, loss)


def solution(mesh):
    in_specs = (P("batch", None, None), P("batch", None, None), P("batch", None), P(None, "head"))
    out_specs = (P("batch", None, None), P("batch", "head"), P())
    return jax.shard_map(
        per_device, mesh=mesh, in_specs=in_specs, out_specs=out_specs, check_vma=False
    )
```

```python
import functools

import jax
import jax.numpy as jnp
from jax import lax
from jax.experimental import pallas as pl
from jax.experimental.pallas import tpu as pltpu
from jax.sharding import PartitionSpec as P

TEACHER_TEMP = 0.07
STUDENT_TEMP = 0.1
EPSILON = 1e-06
LANES = 128
F32 = jnp.float32
BF16 = jnp.bfloat16
MIB = 1 << 20


def kernel_call(body, out_shape, scratch=(), limit=40, scalars=0):
    whole = pl.BlockSpec(memory_space=pltpu.VMEM)

    def call(*args):
        specs = [pl.BlockSpec(memory_space=pltpu.SMEM)] * scalars
        specs += [whole] * (len(args) - scalars)
        return pl.pallas_call(
            body,
            out_shape=out_shape,
            in_specs=specs,
            out_specs=jax.tree.map(lambda _: whole, out_shape),
            scratch_shapes=list(scratch),
            compiler_params=pltpu.CompilerParams(vmem_limit_bytes=limit * MIB),
        )(*args)

    return call


def shape(dims, dtype=F32):
    return jax.ShapeDtypeStruct(dims, dtype)


def picked_unit(patches, positions):
    patch = lax.broadcasted_iota(jnp.int32, (patches.shape[0], positions.shape[1]), 0)
    onehot = (patch == positions).astype(F32).astype(BF16)
    rows = lax.dot_general(
        onehot, patches, (((0,), (0,)), ((), ())), preferred_element_type=F32
    )
    inverse = lax.rsqrt(jnp.sum(rows * rows, axis=1, keepdims=True) + EPSILON)
    return rows * inverse, inverse


def lane_tiles(row, count):
    return jnp.concatenate(
        [jnp.broadcast_to(row[i : i + 1, :], (8, LANES)) for i in range(count)], axis=1
    )


def column(row):
    return jnp.transpose(jnp.broadcast_to(row, (LANES, LANES)))


def fold(block):
    tiles = [block[:, i : i + LANES] for i in range(0, block.shape[1], LANES)]
    while len(tiles) > 1:
        tiles = [a + b for a, b in zip(tiles[::2], tiles[1::2])]
    return tiles[0]


def row_sums(partial):
    total = lax.dot_general(
        jnp.ones((8, LANES), F32),
        partial,
        (((1,), (1,)), ((), ())),
        precision=lax.Precision.HIGHEST,
        preferred_element_type=F32,
    )
    return jnp.concatenate(
        [total[0:1, i : i + LANES] for i in range(0, partial.shape[0], LANES)], axis=0
    )


def col_tiles(total):
    return jnp.concatenate(
        [total[:, i : i + LANES] for i in range(0, total.shape[1], LANES)], axis=0
    )


def split_dot(values, right):
    high = values.astype(BF16)
    low = (values - high.astype(F32)).astype(BF16)
    return jnp.dot(high, right, preferred_element_type=F32) + jnp.dot(
        low, right, preferred_element_type=F32
    )


def teacher_kernel(index_ref, patches_ref, weight_ref, exp_ref, norm_ref, inv_ref, msg_ref):
    wide = weight_ref[...].astype(F32)
    inverse = lax.rsqrt(jnp.sum(wide * wide, axis=0, keepdims=True) + EPSILON)
    inv_ref[...] = inverse
    norm_ref[...] = (wide * inverse).astype(BF16)
    total = jnp.zeros((1, weight_ref.shape[1]), F32)
    for view in range(patches_ref.shape[0]):
        unit, _ = picked_unit(patches_ref[view], index_ref[view : view + 1, :])
        logits = jnp.dot(unit.astype(BF16), norm_ref[...], preferred_element_type=F32)
        block = jnp.exp(logits * (1.0 / TEACHER_TEMP))
        exp_ref[view * LANES : (view + 1) * LANES, :] = block
        total += jnp.sum(block, axis=0, keepdims=True)
    msg_ref[...] = jnp.broadcast_to(col_tiles(total)[None], msg_ref.shape)


def student_kernel(
    index_ref, patches_ref, norm_ref,
    unit_ref, inv_ref, flip_ref, back_ref, logits_ref, exp_ref, part_ref, pull_ref,
    tail,
):
    back_ref[...] = jnp.transpose(norm_ref[...])
    for view in range(patches_ref.shape[0]):
        rows = slice(view * LANES, (view + 1) * LANES)
        unit, inverse = picked_unit(patches_ref[view], index_ref[view : view + 1, :])
        unit_ref[rows, :] = unit
        inv_ref[rows, :] = jnp.broadcast_to(inverse, (LANES, LANES))
        narrow = unit.astype(BF16)
        flip_ref[:, rows] = jnp.transpose(narrow)
        logits = jnp.dot(narrow, norm_ref[...], preferred_element_type=F32)
        block = jnp.exp(logits * (1.0 / STUDENT_TEMP))
        logits_ref[rows, :] = logits
        exp_ref[rows, :] = block
        tail[rows, :] = fold(block)
        pull_ref[rows, :] = split_dot(block, back_ref[...])
    part_ref[...] = row_sums(tail[...])


def row_kernel(has_extra, *refs):
    if has_extra:
        cols_ref, exp_ref, extra_ref, msg_ref, tail = refs
    else:
        cols_ref, exp_ref, msg_ref, tail = refs
    scale = lane_tiles(1.0 / jnp.sum(cols_ref[...], axis=0), cols_ref.shape[1])

    def step(i, carry):
        start = pl.multiple_of(i * 8, 8)
        tail[pl.ds(start, 8), :] = fold(exp_ref[pl.ds(start, 8), :] * scale)
        return carry

    lax.fori_loop(0, exp_ref.shape[0] // 8, step, 0, unroll=8)
    out = row_sums(tail[...])
    if has_extra:
        out = jnp.concatenate([out, extra_ref[...]], axis=0)
    msg_ref[...] = jnp.broadcast_to(out[None], msg_ref.shape)


def col_kernel(has_extra, rows_ref, exp_ref, *refs):
    if has_extra:
        msg_ref, extra_ref, scale_ref = refs
    else:
        msg_ref, scale_ref = refs
    total = jnp.sum(rows_ref[...], axis=0)
    if has_extra:
        extra_ref[...] = total[4:8, :]
    scale = 1.0 / total[0:4, :]
    for j in range(4):
        scale_ref[j * LANES : (j + 1) * LANES, :] = column(scale[j : j + 1, :])
    count = exp_ref.shape[1] // LANES

    def step(i, sums):
        start = pl.multiple_of(i * 8, 8)
        factor = scale_ref[pl.ds(start, 8), :]
        return tuple(
            sums[k] + exp_ref[pl.ds(start, 8), k * LANES : (k + 1) * LANES] * factor
            for k in range(count)
        )

    sums = lax.fori_loop(
        0, exp_ref.shape[0] // 8, step, (jnp.zeros((8, LANES), F32),) * count, unroll=8
    )
    total = jnp.concatenate([jnp.sum(s, axis=0, keepdims=True) for s in sums], axis=0)
    msg_ref[...] = jnp.broadcast_to(total[None], msg_ref.shape)


def last_row_kernel(cols_ref, exp_ref, logits_ref, msg_ref, scale_ref, tail, weighted):
    small = 1.0 / jnp.sum(cols_ref[...], axis=0)
    scale = lane_tiles(small, cols_ref.shape[1])
    scale_ref[...] = scale

    def step(i, carry):
        start = pl.multiple_of(i * 8, 8)
        scaled = exp_ref[pl.ds(start, 8), :] * scale
        tail[pl.ds(start, 8), :] = fold(scaled)
        weighted[pl.ds(start, 8), :] = fold(scaled * logits_ref[pl.ds(start, 8), :])
        return carry

    lax.fori_loop(0, exp_ref.shape[0] // 8, step, 0, unroll=4)
    out = jnp.concatenate([row_sums(tail[...]), row_sums(weighted[...])], axis=0)
    msg_ref[...] = jnp.broadcast_to(out[None], msg_ref.shape)


def pull_kernel(scale_ref, exp_ref, back_ref, pull_ref):
    for j in range(4):
        rows = slice(j * LANES, (j + 1) * LANES)
        pull_ref[j] = split_dot(exp_ref[rows, :] * scale_ref[0:1, :], back_ref[...])


def grad_kernel(
    core_ref, rows_ref, partition_ref, scale_ref, exp_ref, student_ref, flip_ref, weight_ref,
    inv_ref, keep_ref, send_ref, loss_ref, row_scale_ref, factor, softener, logits,
):
    total = jnp.sum(rows_ref[...], axis=0)
    partition = partition_ref[...]
    scale = 1.0 / total[0:4, :]
    row_scale_ref[...] = scale
    losses = jnp.log(partition) - scale * total[4:8, :] * (1.0 / STUDENT_TEMP)
    loss = jnp.sum(jnp.sum(losses, axis=1, keepdims=True), axis=0, keepdims=True)
    loss_ref[...] = jnp.broadcast_to(loss[None], loss_ref.shape)
    softener_rows = 1.0 / partition
    for j in range(4):
        rows = slice(j * LANES, (j + 1) * LANES)
        factor[rows, :] = column(scale[j : j + 1, :])
        softener[rows, :] = column(softener_rows[j : j + 1, :])
    width = logits.shape[1]
    core = core_ref[0]
    wide = (LANES, width)
    for block in range(exp_ref.shape[1] // width):
        cols = slice(block * width, (block + 1) * width)
        for j in range(4):
            rows = slice(j * LANES, (j + 1) * LANES)
            soft = jnp.concatenate([softener[rows, :]] * (width // LANES), axis=1)
            hard = jnp.concatenate([factor[rows, :]] * (width // LANES), axis=1)
            targets = hard * (exp_ref[rows, cols] * scale_ref[0:1, cols])
            logits[rows, :] = (
                (student_ref[rows, cols] * soft - targets) * (1.0 / STUDENT_TEMP)
            ).astype(BF16)
        unit = jnp.dot(flip_ref[...], logits[...], preferred_element_type=F32)
        inverse = inv_ref[:, cols]
        weight_unit = weight_ref[:, cols].astype(F32) * inverse
        inner = jnp.sum(weight_unit * unit, axis=0, keepdims=True)
        full = (inverse * (unit - weight_unit * inner)).reshape(4, 2, 2, 16, width)
        first, second = full[:, :, 0], full[:, :, 1]
        keep_ref[:, :, :, cols] = jnp.where(core == 0, first, second)
        send_ref[:, :, :, cols] = jnp.where(core == 0, second, first)


def exchange(blocks, axis, groups=None):
    return lax.all_to_all(blocks, axis, 0, 0, axis_index_groups=groups)


def share(block, axis, groups, count):
    return exchange(jnp.broadcast_to(block[None], (count,) + block.shape), axis, groups)


def tie(*values):
    return lax.optimization_barrier(values)


def pick(blocks, index):
    return lax.dynamic_index_in_dim(blocks, index, 0, keepdims=False)


def per_device(student_patches, teacher_patches, mask_index, weight):
    view_count, masked_count = mask_index.shape
    feature_dim, columns = weight.shape
    total = view_count * masked_count
    share_rows = feature_dim // 16
    batch_index = lax.axis_index("batch")
    head_index = lax.axis_index("head")
    x_index = batch_index // 4
    z_high = (batch_index // 2) % 2
    core = batch_index % 2
    y_index = head_index % 4
    y_groups = [[4 * z + y for y in range(4)] for z in range(8)]
    z_groups = [[4 * z + y for z in range(8)] for y in range(4)]
    col_msg = shape((16, columns // LANES, LANES))
    row_msg = shape((32, total // LANES, LANES))
    row_msg_two = shape((32, 2 * total // LANES, LANES))
    tail = pltpu.VMEM((total, LANES), F32)

    teacher_exp, weight_norm, weight_inv, cols = kernel_call(
        teacher_kernel,
        (shape((total, columns)), shape((feature_dim, columns), BF16), shape((1, columns)), col_msg),
    )(mask_index, teacher_patches, weight)
    student_patches, cols = tie(student_patches, cols)
    cols = exchange(cols, "batch")

    unit, inverse, flip, back, logits, student_exp, partition_part, student_pull = kernel_call(
        student_kernel,
        (
            shape((total, feature_dim)),
            shape((total, LANES)),
            shape((feature_dim, total), BF16),
            shape((columns, feature_dim), BF16),
            shape((total, columns)),
            shape((total, columns)),
            shape((total // LANES, LANES)),
            shape((total, feature_dim)),
        ),
        [tail],
    )(mask_index, student_patches, weight_norm)

    rows = kernel_call(functools.partial(row_kernel, True), row_msg_two, [tail])(
        cols, teacher_exp, partition_part
    )
    rows = exchange(rows, "head")
    student_piece = lax.psum_scatter(
        student_pull.reshape(4, total // 4, feature_dim), "head", axis_index_groups=y_groups
    )
    cols, partition = kernel_call(
        functools.partial(col_kernel, True), (col_msg, shape((total // LANES, LANES))), [tail]
    )(rows, teacher_exp)
    cols = exchange(cols, "batch")
    cols, student_piece = tie(cols, student_piece)
    student_piece = lax.psum_scatter(
        student_piece.reshape(8, total // 32, feature_dim), "head", axis_index_groups=z_groups
    )
    rows = kernel_call(functools.partial(row_kernel, False), row_msg, [tail])(cols, teacher_exp)
    rows = exchange(rows, "head")
    cols = kernel_call(functools.partial(col_kernel, False), col_msg, [tail])(rows, teacher_exp)
    cols = exchange(cols, "batch")
    cols, student_piece = tie(cols, student_piece)

    rows, col_scale = kernel_call(
        last_row_kernel, (row_msg_two, shape((8, columns))), [tail, tail]
    )(cols, teacher_exp, logits)
    rows = exchange(rows, "head")
    teacher_pull = kernel_call(pull_kernel, shape((4, total // 4, feature_dim)))(
        col_scale, teacher_exp, back
    )
    piece = pick(teacher_pull, y_index)
    for step in (1, 2, 3):
        pairs = [(i, i // 4 * 4 + (i + step) % 4) for i in range(32)]
        piece = piece + lax.ppermute(pick(teacher_pull, (y_index + step) % 4), "head", pairs)
    rows, piece = tie(rows, piece)

    part = shape((4, 2, share_rows, columns))
    keep, send, loss_part, row_scale = kernel_call(
        grad_kernel,
        (part, part, shape((1, 1, LANES)), shape((total // LANES, LANES))),
        [tail, tail, pltpu.VMEM((total, 512), BF16)],
        scalars=1,
    )(
        core.reshape(1), rows, partition, col_scale, teacher_exp, student_exp, flip, weight,
        weight_inv,
    )
    parts = keep + lax.ppermute(send, "batch", [(i, i ^ 1) for i in range(16)])
    held = pick(parts, x_index)
    for step in (1, 2, 3):
        pairs = [(i, (i + 4 * step) % 16) for i in range(16)]
        held = held + lax.ppermute(pick(parts, (x_index + step) % 4), "batch", pairs)

    piece = jnp.sum(
        exchange(piece.reshape(8, total // 32, feature_dim), "head", z_groups), axis=0
    )
    first = y_index * (total // 4) + (head_index // 4) * (total // 32)

    def cut(values):
        return lax.dynamic_slice_in_dim(values, first, total // 32, 0)

    piece = (
        student_piece / cut(partition.reshape(-1))[:, None]
        - piece * cut(row_scale.reshape(-1))[:, None]
    ) * (1.0 / STUDENT_TEMP)
    unit_piece = cut(unit)
    inner = jnp.sum(unit_piece * piece, axis=1, keepdims=True)
    piece = cut(inverse)[:, 0:1] * (piece - unit_piece * inner)
    piece = share(piece, "head", z_groups, 8).reshape(total // 4, feature_dim)
    piece, held = tie(piece, held)
    keep, send = pick(held, z_high), pick(held, 1 - z_high)
    grad_weight = keep + lax.ppermute(send, "batch", [(i, i ^ 2) for i in range(16)])
    grad_rows = share(piece, "head", y_groups, 4).reshape(view_count, masked_count, feature_dim)
    losses = share(loss_part[0], "batch", None, 16)
    loss = jnp.sum(losses, axis=0)[0, 0] / (total * lax.axis_size("batch"))
    return (grad_rows, grad_weight, loss)


def solution(mesh):
    in_specs = (P("batch", None, None), P("batch", None, None), P("batch", None), P(None, "head"))
    out_specs = (P("batch", None, None), P("batch", "head"), P())
    return jax.shard_map(
        per_device, mesh=mesh, in_specs=in_specs, out_specs=out_specs, check_vma=False
    )
```

```python
import functools

import jax
import jax.numpy as jnp
from jax import lax
from jax.experimental import pallas as pl
from jax.experimental.pallas import tpu as pltpu
from jax.sharding import PartitionSpec as P

TEACHER_TEMP = 0.07
STUDENT_TEMP = 0.1
EPSILON = 1e-06
LANES = 128
F32 = jnp.float32
BF16 = jnp.bfloat16
MIB = 1 << 20


def kernel_call(body, out_shape, scratch=(), limit=12, scalars=0, far=0):
    whole = pl.BlockSpec(memory_space=pltpu.VMEM)

    def call(*args):
        specs = [pl.BlockSpec(memory_space=pltpu.SMEM)] * scalars
        specs += [pl.BlockSpec(memory_space=pltpu.HBM)] * far
        specs += [whole] * (len(args) - scalars - far)
        return pl.pallas_call(
            body,
            out_shape=out_shape,
            in_specs=specs,
            out_specs=jax.tree.map(lambda _: whole, out_shape),
            scratch_shapes=list(scratch),
            compiler_params=pltpu.CompilerParams(vmem_limit_bytes=limit * MIB),
        )(*args)

    return call


def shape(dims, dtype=F32):
    return jax.ShapeDtypeStruct(dims, dtype)


def picked_unit(patches, positions):
    patch = lax.broadcasted_iota(jnp.int32, (patches.shape[0], positions.shape[1]), 0)
    onehot = (patch == positions).astype(F32).astype(BF16)
    rows = lax.dot_general(
        onehot, patches, (((0,), (0,)), ((), ())), preferred_element_type=F32
    )
    inverse = lax.rsqrt(jnp.sum(rows * rows, axis=1, keepdims=True) + EPSILON)
    return rows * inverse, inverse


def far_off(array):
    return pltpu.with_memory_space_constraint(array, pltpu.HBM)


def lane_tiles(row, count):
    return jnp.concatenate(
        [jnp.broadcast_to(row[i : i + 1, :], (8, LANES)) for i in range(count)], axis=1
    )


def column(row):
    return jnp.transpose(jnp.broadcast_to(row, (LANES, LANES)))


def fold(block):
    tiles = [block[:, i : i + LANES] for i in range(0, block.shape[1], LANES)]
    while len(tiles) > 1:
        tiles = [a + b for a, b in zip(tiles[::2], tiles[1::2])]
    return tiles[0]


def row_sums(partial):
    total = lax.dot_general(
        jnp.ones((8, LANES), F32),
        partial,
        (((1,), (1,)), ((), ())),
        precision=lax.Precision.HIGHEST,
        preferred_element_type=F32,
    )
    return jnp.concatenate(
        [total[0:1, i : i + LANES] for i in range(0, partial.shape[0], LANES)], axis=0
    )


def col_tiles(total):
    return jnp.concatenate(
        [total[:, i : i + LANES] for i in range(0, total.shape[1], LANES)], axis=0
    )


def start_kernel(
    places_ref, weight_hbm, teacher_hbm, student_hbm, index_ref,
    back_ref, inv_ref, teacher_exp_ref, msg_ref,
    own_unit_ref, own_inv_ref, flip_ref, logits_ref, student_exp_ref, part_ref,
    weight_ref, teacher_ref, student_ref, norm_ref, unit_ref, row_inv_ref, tail, sems,
):
    copies = [
        pltpu.make_async_copy(source, target, sems.at[i])
        for i, (source, target) in enumerate(
            [(weight_hbm, weight_ref), (teacher_hbm, teacher_ref), (student_hbm, student_ref)]
        )
    ]
    for copy in copies:
        copy.start()
    copies[0].wait()
    wide = weight_ref[...].astype(F32)
    inverse = lax.rsqrt(jnp.sum(wide * wide, axis=0, keepdims=True) + EPSILON)
    inv_ref[...] = inverse
    norm_ref[...] = (wide * inverse).astype(BF16)
    back_ref[...] = jnp.transpose(norm_ref[...])
    copies[1].wait()
    total = jnp.zeros((1, weight_ref.shape[1]), F32)
    for view in range(teacher_ref.shape[0]):
        unit, _ = picked_unit(teacher_ref[view], index_ref[view : view + 1, :])
        logits = jnp.dot(unit.astype(BF16), norm_ref[...], preferred_element_type=F32)
        block = jnp.exp(logits * (1.0 / TEACHER_TEMP))
        teacher_exp_ref[view * LANES : (view + 1) * LANES, :] = block
        total += jnp.sum(block, axis=0, keepdims=True)
    msg_ref[...] = jnp.broadcast_to(col_tiles(total)[None], msg_ref.shape)
    copies[2].wait()
    for view in range(student_ref.shape[0]):
        rows = slice(view * LANES, (view + 1) * LANES)
        unit, inverse = picked_unit(student_ref[view], index_ref[view : view + 1, :])
        unit_ref[rows, :] = unit
        row_inv_ref[rows, :] = jnp.broadcast_to(inverse, (LANES, LANES))
        narrow = unit.astype(BF16)
        flip_ref[:, rows] = jnp.transpose(narrow)
        logits = jnp.dot(narrow, norm_ref[...], preferred_element_type=F32)
        block = jnp.exp(logits * (1.0 / STUDENT_TEMP))
        logits_ref[rows, :] = logits
        student_exp_ref[rows, :] = block
        tail[rows, :] = fold(block)
    part_ref[...] = row_sums(tail[...])
    own = pl.ds(pl.multiple_of(places_ref[3], 16), own_unit_ref.shape[0])
    own_unit_ref[...] = unit_ref[own, :]
    own_inv_ref[...] = row_inv_ref[own, :]


def row_kernel(has_extra, *refs):
    if has_extra:
        cols_ref, exp_ref, extra_ref, msg_ref, tail = refs
    else:
        cols_ref, exp_ref, msg_ref, tail = refs
    scale = lane_tiles(1.0 / jnp.sum(cols_ref[...], axis=0), cols_ref.shape[1])

    def step(i, carry):
        start = pl.multiple_of(i * 8, 8)
        tail[pl.ds(start, 8), :] = fold(exp_ref[pl.ds(start, 8), :] * scale)
        return carry

    lax.fori_loop(0, exp_ref.shape[0] // 8, step, 0, unroll=8)
    out = row_sums(tail[...])
    if has_extra:
        out = jnp.concatenate([out, extra_ref[...]], axis=0)
    msg_ref[...] = jnp.broadcast_to(out[None], msg_ref.shape)


def col_kernel(has_extra, rows_ref, exp_ref, *refs):
    if has_extra:
        msg_ref, extra_ref, scale_ref = refs
    else:
        msg_ref, scale_ref = refs
    total = jnp.sum(rows_ref[...], axis=0)
    if has_extra:
        extra_ref[...] = total[4:8, :]
    scale = 1.0 / total[0:4, :]
    for j in range(4):
        scale_ref[j * LANES : (j + 1) * LANES, :] = column(scale[j : j + 1, :])
    count = exp_ref.shape[1] // LANES

    def step(i, sums):
        start = pl.multiple_of(i * 8, 8)
        factor = scale_ref[pl.ds(start, 8), :]
        return tuple(
            sums[k] + exp_ref[pl.ds(start, 8), k * LANES : (k + 1) * LANES] * factor
            for k in range(count)
        )

    sums = lax.fori_loop(
        0, exp_ref.shape[0] // 8, step, (jnp.zeros((8, LANES), F32),) * count, unroll=8
    )
    total = jnp.concatenate([jnp.sum(s, axis=0, keepdims=True) for s in sums], axis=0)
    msg_ref[...] = jnp.broadcast_to(total[None], msg_ref.shape)


def last_row_kernel(cols_ref, exp_ref, logits_ref, msg_ref, scale_ref, tail, weighted):
    small = 1.0 / jnp.sum(cols_ref[...], axis=0)
    scale = lane_tiles(small, cols_ref.shape[1])
    scale_ref[...] = scale

    def step(i, carry):
        start = pl.multiple_of(i * 8, 8)
        scaled = exp_ref[pl.ds(start, 8), :] * scale
        tail[pl.ds(start, 8), :] = fold(scaled)
        weighted[pl.ds(start, 8), :] = fold(scaled * logits_ref[pl.ds(start, 8), :])
        return carry

    lax.fori_loop(0, exp_ref.shape[0] // 8, step, 0, unroll=4)
    out = jnp.concatenate([row_sums(tail[...]), row_sums(weighted[...])], axis=0)
    msg_ref[...] = jnp.broadcast_to(out[None], msg_ref.shape)


def grad_kernel(
    places_ref, rows_ref, partition_ref, scale_ref, exp_ref, student_ref, flip_ref, back_ref,
    weight_ref, inv_ref, keep_ref, send_ref, pull_ref, factor, softener, logits,
):
    total = jnp.sum(rows_ref[...], axis=0)
    partition = partition_ref[...]
    scale = 1.0 / total[0:4, :]
    losses = jnp.log(partition) - scale * total[4:8, :] * (1.0 / STUDENT_TEMP)
    loss = jnp.sum(jnp.sum(losses, axis=1, keepdims=True), axis=0, keepdims=True)
    columns = exp_ref.shape[1]
    for ref in (keep_ref, send_ref):
        ref[:, :, :, columns:] = jnp.broadcast_to(loss[None, None], ref.shape[:3] + (LANES,))
    softener_rows = 1.0 / partition
    for j in range(4):
        rows = slice(j * LANES, (j + 1) * LANES)
        factor[rows, :] = column(scale[j : j + 1, :])
        softener[rows, :] = column(softener_rows[j : j + 1, :])
    width = logits.shape[1]
    core, x_index, z_high = places_ref[0], places_ref[1], places_ref[2]
    wide = (LANES, width)
    for block in range(columns // width):
        cols = slice(block * width, (block + 1) * width)
        for j in range(4):
            rows = slice(j * LANES, (j + 1) * LANES)
            soft = jnp.concatenate([softener[rows, :]] * (width // LANES), axis=1)
            hard = jnp.concatenate([factor[rows, :]] * (width // LANES), axis=1)
            targets = hard * (exp_ref[rows, cols] * scale_ref[0:1, cols])
            logits[rows, :] = (
                (student_ref[rows, cols] * soft - targets) * (1.0 / STUDENT_TEMP)
            ).astype(BF16)
        pull = jnp.dot(logits[...], back_ref[cols, :], preferred_element_type=F32)
        pull = pull.reshape(pull_ref.shape)
        pull_ref[...] = pull if block == 0 else pull_ref[...] + pull
        unit = jnp.dot(flip_ref[...], logits[...], preferred_element_type=F32)
        inverse = inv_ref[:, cols]
        weight_unit = weight_ref[:, cols].astype(F32) * inverse
        inner = jnp.sum(weight_unit * unit, axis=0, keepdims=True)
        full = (inverse * (unit - weight_unit * inner)).reshape(4, 2, 2, 16, width)
        first, second = full[:, :, 0], full[:, :, 1]
        for x in range(4):
            for z in range(2):
                place = ((x - x_index) & 3, z ^ z_high)
                keep_ref[place + (slice(None), cols)] = jnp.where(
                    core == 0, first[x, z], second[x, z]
                )
                send_ref[place + (slice(None), cols)] = jnp.where(
                    core == 0, second[x, z], first[x, z]
                )


def finish_kernel(blocks_ref, unit_ref, inv_ref, copies_ref):
    pull = jnp.sum(blocks_ref[...], axis=0)
    unit = unit_ref[...]
    inner = jnp.sum(unit * pull, axis=1, keepdims=True)
    rows = inv_ref[:, 0:1] * (pull - unit * inner)
    copies_ref[...] = jnp.broadcast_to(rows[None], copies_ref.shape)


def exchange(blocks, axis, groups=None):
    return lax.all_to_all(blocks, axis, 0, 0, axis_index_groups=groups)


def share(block, axis, groups, count):
    return exchange(jnp.broadcast_to(block[None], (count,) + block.shape), axis, groups)


def tie(*values):
    return lax.optimization_barrier(values)


def per_device(student_patches, teacher_patches, mask_index, weight):
    view_count, masked_count = mask_index.shape
    feature_dim, columns = weight.shape
    total = view_count * masked_count
    share_rows = feature_dim // 16
    batch_index = lax.axis_index("batch")
    head_index = lax.axis_index("head")
    first = (head_index & 3) * (total // 4) + (head_index >> 2) * (total // 32)
    places = jnp.stack([batch_index & 1, batch_index >> 2, (batch_index >> 1) & 1, first])
    y_groups = [[4 * z + y for y in range(4)] for z in range(8)]
    z_groups = [[4 * z + y for z in range(8)] for y in range(4)]
    col_msg = shape((16, columns // LANES, LANES))
    row_msg = shape((32, total // LANES, LANES))
    row_msg_two = shape((32, 2 * total // LANES, LANES))
    tail = pltpu.VMEM((total, LANES), F32)

    (
        back, weight_inv, teacher_exp, cols,
        unit, inverse, flip, logits, student_exp, partition_part,
    ) = kernel_call(
        start_kernel,
        (
            shape((columns, feature_dim), BF16),
            shape((1, columns)),
            shape((total, columns)),
            col_msg,
            shape((total // 32, feature_dim)),
            shape((total // 32, LANES)),
            shape((feature_dim, total), BF16),
            shape((total, columns)),
            shape((total, columns)),
            shape((total // LANES, LANES)),
        ),
        [
            pltpu.VMEM(weight.shape, BF16),
            pltpu.VMEM(teacher_patches.shape, BF16),
            pltpu.VMEM(student_patches.shape, BF16),
            pltpu.VMEM((feature_dim, columns), BF16),
            pltpu.VMEM((total, feature_dim), F32),
            tail,
            tail,
            pltpu.SemaphoreType.DMA((3,)),
        ],
        scalars=1,
        far=3,
        limit=16,
    )(
        places, far_off(weight), far_off(teacher_patches), far_off(student_patches), mask_index
    )
    cols = exchange(cols, "batch")
    rows = kernel_call(functools.partial(row_kernel, True), row_msg_two, [tail])(
        cols, teacher_exp, partition_part
    )
    rows = exchange(rows, "head")
    cols, partition = kernel_call(
        functools.partial(col_kernel, True), (col_msg, shape((total // LANES, LANES))), [tail]
    )(rows, teacher_exp)
    cols = exchange(cols, "batch")
    rows = kernel_call(functools.partial(row_kernel, False), row_msg, [tail])(cols, teacher_exp)
    rows = exchange(rows, "head")
    cols = kernel_call(functools.partial(col_kernel, False), col_msg, [tail])(rows, teacher_exp)
    cols = exchange(cols, "batch")
    rows, col_scale = kernel_call(
        last_row_kernel, (row_msg_two, shape((8, columns))), [tail, tail]
    )(cols, teacher_exp, logits)
    rows = exchange(rows, "head")

    part = shape((4, 2, share_rows, columns + LANES))
    keep, send, pull = kernel_call(
        grad_kernel,
        (part, part, shape((4, total // 4, feature_dim))),
        [tail, tail, pltpu.VMEM((total, 512), BF16)],
        scalars=1,
        limit=16,
    )(
        places, rows, partition, col_scale, teacher_exp, student_exp, flip, back, weight,
        weight_inv,
    )
    parts = keep + lax.ppermute(send, "batch", [(i, i ^ 1) for i in range(16)])
    parts, pull = tie(parts, pull)
    piece = jnp.sum(exchange(pull, "head", y_groups), axis=0)

    held = parts[0]
    for step in (1, 2, 3):
        pairs = [(i, (i + 4 * step) % 16) for i in range(16)]
        held = held + lax.ppermute(parts[step], "batch", pairs)

    piece = kernel_call(finish_kernel, shape((8, total // 32, feature_dim)))(
        exchange(piece.reshape(8, total // 32, feature_dim), "head", z_groups), unit, inverse
    )
    piece = exchange(piece, "head", z_groups).reshape(total // 4, feature_dim)
    grad_weight = held[0] + lax.ppermute(held[1], "batch", [(i, i ^ 2) for i in range(16)])
    grad_rows = share(piece, "head", y_groups, 4).reshape(view_count, masked_count, feature_dim)
    loss = grad_weight[0, columns] / (total * lax.axis_size("batch"))
    return (grad_rows, grad_weight[:, :columns], loss)


def solution(mesh):
    in_specs = (P("batch", None, None), P("batch", None, None), P("batch", None), P(None, "head"))
    out_specs = (P("batch", None, None), P("batch", "head"), P())
    return jax.shard_map(
        per_device, mesh=mesh, in_specs=in_specs, out_specs=out_specs, check_vma=False
    )
```

```python
import functools

import jax
import jax.numpy as jnp
from jax import lax
from jax.experimental import pallas as pl
from jax.experimental.pallas import tpu as pltpu
from jax.sharding import PartitionSpec as P

TEACHER_TEMP = 0.07
STUDENT_TEMP = 0.1
EPSILON = 1e-06
LOG2_E = 1.4426950408889634
LANES = 128
F32 = jnp.float32
BF16 = jnp.bfloat16
MIB = 1 << 20


def kernel_call(body, out_shape, scratch=(), limit=12, scalars=0, far=0):
    whole = pl.BlockSpec(memory_space=pltpu.VMEM)

    def call(*args):
        specs = [pl.BlockSpec(memory_space=pltpu.SMEM)] * scalars
        specs += [pl.BlockSpec(memory_space=pltpu.HBM)] * far
        specs += [whole] * (len(args) - scalars - far)
        return pl.pallas_call(
            body,
            out_shape=out_shape,
            in_specs=specs,
            out_specs=jax.tree.map(lambda _: whole, out_shape),
            scratch_shapes=list(scratch),
            compiler_params=pltpu.CompilerParams(vmem_limit_bytes=limit * MIB),
        )(*args)

    return call


def shape(dims, dtype=F32):
    return jax.ShapeDtypeStruct(dims, dtype)


def picked_unit(patches, positions):
    patch = lax.broadcasted_iota(jnp.int32, (patches.shape[0], positions.shape[1]), 0)
    onehot = (patch == positions).astype(F32).astype(BF16)
    rows = lax.dot_general(
        onehot, patches, (((0,), (0,)), ((), ())), preferred_element_type=F32
    )
    inverse = lax.rsqrt(jnp.sum(rows * rows, axis=1, keepdims=True) + EPSILON)
    return rows * inverse, inverse


def far_off(array):
    return pltpu.with_memory_space_constraint(array, pltpu.HBM)


def lane_tiles(row, count):
    return jnp.concatenate(
        [jnp.broadcast_to(row[i : i + 1, :], (8, LANES)) for i in range(count)], axis=1
    )


def column(row):
    return jnp.transpose(jnp.broadcast_to(row, (LANES, LANES)))


def fold(block):
    tiles = [block[:, i : i + LANES] for i in range(0, block.shape[1], LANES)]
    while len(tiles) > 1:
        tiles = [a + b for a, b in zip(tiles[::2], tiles[1::2])]
    return tiles[0]


def row_sums(partial):
    total = lax.dot_general(
        jnp.ones((8, LANES), F32),
        partial,
        (((1,), (1,)), ((), ())),
        precision=lax.Precision.HIGHEST,
        preferred_element_type=F32,
    )
    return jnp.concatenate(
        [total[0:1, i : i + LANES] for i in range(0, partial.shape[0], LANES)], axis=0
    )


def col_tiles(total):
    return jnp.concatenate(
        [total[:, i : i + LANES] for i in range(0, total.shape[1], LANES)], axis=0
    )


def start_kernel(
    places_ref, weight_hbm, teacher_hbm, student_hbm, index_hbm,
    back_ref, inv_ref, teacher_exp_ref, msg_ref,
    own_unit_ref, own_inv_ref, flip_ref, logits_ref, student_exp_ref, part_ref,
    weight_ref, teacher_ref, student_ref, index_ref, norm_ref, unit_ref, row_inv_ref, tail, sems,
):
    copies = [
        pltpu.make_async_copy(source, target, sems.at[i])
        for i, (source, target) in enumerate(
            [
                (weight_hbm, weight_ref),
                (index_hbm, index_ref),
                (teacher_hbm, teacher_ref),
                (student_hbm, student_ref),
            ]
        )
    ]
    for copy in copies:
        copy.start()
    copies[0].wait()
    wide = weight_ref[...].astype(F32)
    inverse = lax.rsqrt(jnp.sum(wide * wide, axis=0, keepdims=True) + EPSILON)
    inv_ref[...] = inverse
    norm_ref[...] = (wide * inverse).astype(BF16)
    back_ref[...] = jnp.transpose(norm_ref[...])
    copies[1].wait()
    copies[2].wait()
    total = jnp.zeros((1, weight_ref.shape[1]), F32)
    for view in range(teacher_ref.shape[0]):
        unit, _ = picked_unit(teacher_ref[view], index_ref[view : view + 1, :])
        logits = jnp.dot(unit.astype(BF16), norm_ref[...], preferred_element_type=F32)
        block = jnp.exp2(logits * (LOG2_E / TEACHER_TEMP))
        teacher_exp_ref[view * LANES : (view + 1) * LANES, :] = block
        total += jnp.sum(block, axis=0, keepdims=True)
    msg_ref[...] = col_tiles(total)
    copies[3].wait()
    for view in range(student_ref.shape[0]):
        rows = slice(view * LANES, (view + 1) * LANES)
        unit, inverse = picked_unit(student_ref[view], index_ref[view : view + 1, :])
        unit_ref[rows, :] = unit
        row_inv_ref[rows, :] = jnp.broadcast_to(inverse, (LANES, LANES))
        narrow = unit.astype(BF16)
        flip_ref[:, rows] = jnp.transpose(narrow)
        logits = jnp.dot(narrow, norm_ref[...], preferred_element_type=F32)
        block = jnp.exp2(logits * (LOG2_E / STUDENT_TEMP))
        logits_ref[rows, :] = logits
        student_exp_ref[rows, :] = block
        tail[rows, :] = fold(block)
    part_ref[...] = row_sums(tail[...])
    own = pl.ds(pl.multiple_of(places_ref[3], 16), own_unit_ref.shape[0])
    own_unit_ref[...] = unit_ref[own, :]
    own_inv_ref[...] = row_inv_ref[own, :]


def row_kernel(has_extra, *refs):
    if has_extra:
        cols_ref, exp_ref, extra_ref, msg_ref, tail = refs
    else:
        cols_ref, exp_ref, msg_ref, tail = refs
    scale = lane_tiles(1.0 / jnp.sum(cols_ref[...], axis=0), cols_ref.shape[1])

    def step(i, carry):
        start = pl.multiple_of(i * 8, 8)
        tail[pl.ds(start, 8), :] = fold(exp_ref[pl.ds(start, 8), :] * scale)
        return carry

    lax.fori_loop(0, exp_ref.shape[0] // 8, step, 0, unroll=8)
    out = row_sums(tail[...])
    if has_extra:
        out = jnp.concatenate([out, extra_ref[...]], axis=0)
    msg_ref[...] = jnp.broadcast_to(out[None], msg_ref.shape)


def col_kernel(has_extra, rows_ref, exp_ref, *refs):
    if has_extra:
        msg_ref, extra_ref, scale_ref = refs
    else:
        msg_ref, scale_ref = refs
    total = jnp.sum(rows_ref[...], axis=0)
    if has_extra:
        extra_ref[...] = total[4:8, :]
    scale = 1.0 / total[0:4, :]
    for j in range(4):
        scale_ref[j * LANES : (j + 1) * LANES, :] = column(scale[j : j + 1, :])
    count = exp_ref.shape[1] // LANES

    def step(i, sums):
        start = pl.multiple_of(i * 8, 8)
        factor = scale_ref[pl.ds(start, 8), :]
        return tuple(
            sums[k] + exp_ref[pl.ds(start, 8), k * LANES : (k + 1) * LANES] * factor
            for k in range(count)
        )

    sums = lax.fori_loop(
        0, exp_ref.shape[0] // 8, step, (jnp.zeros((8, LANES), F32),) * count, unroll=8
    )
    msg_ref[...] = jnp.concatenate([jnp.sum(s, axis=0, keepdims=True) for s in sums], axis=0)


def last_row_kernel(cols_ref, exp_ref, logits_ref, msg_ref, scale_ref, tail, weighted):
    small = 1.0 / jnp.sum(cols_ref[...], axis=0)
    scale = lane_tiles(small, cols_ref.shape[1])
    scale_ref[...] = scale

    def step(i, carry):
        start = pl.multiple_of(i * 8, 8)
        scaled = exp_ref[pl.ds(start, 8), :] * scale
        tail[pl.ds(start, 8), :] = fold(scaled)
        weighted[pl.ds(start, 8), :] = fold(scaled * logits_ref[pl.ds(start, 8), :])
        return carry

    lax.fori_loop(0, exp_ref.shape[0] // 8, step, 0, unroll=4)
    out = jnp.concatenate([row_sums(tail[...]), row_sums(weighted[...])], axis=0)
    msg_ref[...] = jnp.broadcast_to(out[None], msg_ref.shape)


def grad_kernel(
    places_ref, rows_ref, partition_ref, scale_ref, exp_ref, student_ref, flip_ref, back_ref,
    weight_ref, inv_ref, keep_ref, send_ref, pull_ref, factor, softener, logits,
):
    total = jnp.sum(rows_ref[...], axis=0)
    partition = partition_ref[...]
    scale = 1.0 / total[0:4, :]
    losses = jnp.log(partition) - scale * total[4:8, :] * (1.0 / STUDENT_TEMP)
    loss = jnp.sum(jnp.sum(losses, axis=1, keepdims=True), axis=0, keepdims=True)
    columns = exp_ref.shape[1]
    for ref in (keep_ref, send_ref):
        ref[:, :, :, columns:] = jnp.broadcast_to(loss[None, None], ref.shape[:3] + (LANES,))
    softener_rows = 1.0 / partition
    for j in range(4):
        rows = slice(j * LANES, (j + 1) * LANES)
        factor[rows, :] = column(scale[j : j + 1, :])
        softener[rows, :] = column(softener_rows[j : j + 1, :])
    width = logits.shape[1]
    core, x_index, z_high = places_ref[0], places_ref[1], places_ref[2]
    wide = (LANES, width)
    for block in range(columns // width):
        cols = slice(block * width, (block + 1) * width)
        for j in range(4):
            rows = slice(j * LANES, (j + 1) * LANES)
            soft = jnp.concatenate([softener[rows, :]] * (width // LANES), axis=1)
            hard = jnp.concatenate([factor[rows, :]] * (width // LANES), axis=1)
            targets = hard * (exp_ref[rows, cols] * scale_ref[0:1, cols])
            logits[rows, :] = (
                (student_ref[rows, cols] * soft - targets) * (1.0 / STUDENT_TEMP)
            ).astype(BF16)
        pull = jnp.dot(logits[...], back_ref[cols, :], preferred_element_type=F32)
        pull = pull.reshape(pull_ref.shape)
        pull_ref[...] = pull if block == 0 else pull_ref[...] + pull
        unit = jnp.dot(flip_ref[...], logits[...], preferred_element_type=F32)
        inverse = inv_ref[:, cols]
        weight_unit = weight_ref[:, cols].astype(F32) * inverse
        inner = jnp.sum(weight_unit * unit, axis=0, keepdims=True)
        full = (inverse * (unit - weight_unit * inner)).reshape(4, 2, 2, 16, width)
        first, second = full[:, :, 0], full[:, :, 1]
        for x in range(4):
            for z in range(2):
                place = ((x - x_index) & 3, z ^ z_high)
                keep_ref[place + (slice(None), cols)] = jnp.where(
                    core == 0, first[x, z], second[x, z]
                )
                send_ref[place + (slice(None), cols)] = jnp.where(
                    core == 0, second[x, z], first[x, z]
                )


def pair_kernel(pair_ref, copies_ref):
    copies_ref[...] = jnp.broadcast_to(jnp.sum(pair_ref[...], axis=0)[None], copies_ref.shape)


def finish_kernel(blocks_ref, unit_ref, inv_ref, copies_ref):
    pull = jnp.sum(blocks_ref[...], axis=0)
    unit = unit_ref[...]
    inner = jnp.sum(unit * pull, axis=1, keepdims=True)
    rows = inv_ref[:, 0:1] * (pull - unit * inner)
    copies_ref[...] = jnp.broadcast_to(rows[None], copies_ref.shape)


def exchange(blocks, axis, groups=None):
    return lax.all_to_all(blocks, axis, 0, 0, axis_index_groups=groups)


def share(block, axis, groups, count):
    return exchange(jnp.broadcast_to(block[None], (count,) + block.shape), axis, groups)


def over_batch(block):
    pairs = [[i, i + 1] for i in range(0, 16, 2)]
    rest = [[i for i in range(16) if i % 2 == core] for core in range(2)]
    both = lax.all_gather(block, "batch", axis_index_groups=pairs)
    copies = kernel_call(pair_kernel, shape((8,) + block.shape), limit=4)(both)
    return exchange(copies, "batch", rest)


def tie(*values):
    return lax.optimization_barrier(values)


def per_device(student_patches, teacher_patches, mask_index, weight):
    view_count, masked_count = mask_index.shape
    feature_dim, columns = weight.shape
    total = view_count * masked_count
    share_rows = feature_dim // 16
    batch_index = lax.axis_index("batch")
    head_index = lax.axis_index("head")
    first = (head_index & 3) * (total // 4) + (head_index >> 2) * (total // 32)
    places = jnp.stack([batch_index & 1, batch_index >> 2, (batch_index >> 1) & 1, first])
    y_groups = [[4 * z + y for y in range(4)] for z in range(8)]
    z_groups = [[4 * z + y for z in range(8)] for y in range(4)]
    col_msg = shape((columns // LANES, LANES))
    row_msg = shape((32, total // LANES, LANES))
    row_msg_two = shape((32, 2 * total // LANES, LANES))
    tail = pltpu.VMEM((total, LANES), F32)

    (
        back, weight_inv, teacher_exp, cols,
        unit, inverse, flip, logits, student_exp, partition_part,
    ) = kernel_call(
        start_kernel,
        (
            shape((columns, feature_dim), BF16),
            shape((1, columns)),
            shape((total, columns)),
            col_msg,
            shape((total // 32, feature_dim)),
            shape((total // 32, LANES)),
            shape((feature_dim, total), BF16),
            shape((total, columns)),
            shape((total, columns)),
            shape((total // LANES, LANES)),
        ),
        [
            pltpu.VMEM(weight.shape, BF16),
            pltpu.VMEM(teacher_patches.shape, BF16),
            pltpu.VMEM(student_patches.shape, BF16),
            pltpu.VMEM(mask_index.shape, jnp.int32),
            pltpu.VMEM((feature_dim, columns), BF16),
            pltpu.VMEM((total, feature_dim), F32),
            tail,
            tail,
            pltpu.SemaphoreType.DMA((4,)),
        ],
        scalars=1,
        far=4,
        limit=16,
    )(
        places, far_off(weight), far_off(teacher_patches), far_off(student_patches),
        far_off(mask_index),
    )
    cols = over_batch(cols)
    rows = kernel_call(functools.partial(row_kernel, True), row_msg_two, [tail])(
        cols, teacher_exp, partition_part
    )
    rows = exchange(rows, "head")
    cols, partition = kernel_call(
        functools.partial(col_kernel, True), (col_msg, shape((total // LANES, LANES))), [tail]
    )(rows, teacher_exp)
    cols = over_batch(cols)
    rows = kernel_call(functools.partial(row_kernel, False), row_msg, [tail])(cols, teacher_exp)
    rows = exchange(rows, "head")
    cols = kernel_call(functools.partial(col_kernel, False), col_msg, [tail])(rows, teacher_exp)
    cols = over_batch(cols)
    rows, col_scale = kernel_call(
        last_row_kernel, (row_msg_two, shape((8, columns))), [tail, tail]
    )(cols, teacher_exp, logits)
    rows = exchange(rows, "head")

    part = shape((4, 2, share_rows, columns + LANES))
    keep, send, pull = kernel_call(
        grad_kernel,
        (part, part, shape((4, total // 4, feature_dim))),
        [tail, tail, pltpu.VMEM((total, 512), BF16)],
        scalars=1,
        limit=16,
    )(
        places, rows, partition, col_scale, teacher_exp, student_exp, flip, back, weight,
        weight_inv,
    )
    parts = keep + lax.ppermute(send, "batch", [(i, i ^ 1) for i in range(16)])
    parts, pull = tie(parts, pull)
    piece = jnp.sum(exchange(pull, "head", y_groups), axis=0)

    held = parts[0]
    for step in (1, 2, 3):
        pairs = [(i, (i + 4 * step) % 16) for i in range(16)]
        held = held + lax.ppermute(parts[step], "batch", pairs)

    piece = kernel_call(finish_kernel, shape((8, total // 32, feature_dim)))(
        exchange(piece.reshape(8, total // 32, feature_dim), "head", z_groups), unit, inverse
    )
    piece = exchange(piece, "head", z_groups).reshape(total // 4, feature_dim)
    grad_weight = held[0] + lax.ppermute(held[1], "batch", [(i, i ^ 2) for i in range(16)])
    grad_rows = share(piece, "head", y_groups, 4).reshape(view_count, masked_count, feature_dim)
    loss = grad_weight[0, columns] / (total * lax.axis_size("batch"))
    return (grad_rows, grad_weight[:, :columns], loss)


def solution(mesh):
    in_specs = (P("batch", None, None), P("batch", None, None), P("batch", None), P(None, "head"))
    out_specs = (P("batch", None, None), P("batch", "head"), P())
    return jax.shard_map(
        per_device, mesh=mesh, in_specs=in_specs, out_specs=out_specs, check_vma=False
    )
```

```python
import functools

import jax
import jax.numpy as jnp
from jax import lax
from jax.experimental import pallas as pl
from jax.experimental.pallas import tpu as pltpu
from jax.sharding import PartitionSpec as P

TEACHER_TEMP = 0.07
STUDENT_TEMP = 0.1
EPSILON = 1e-06
LOG2_E = 1.4426950408889634
LANES = 128
F32 = jnp.float32
BF16 = jnp.bfloat16
MIB = 1 << 20


def kernel_call(body, out_shape, scratch=(), limit=12, scalars=0, far=0):
    whole = pl.BlockSpec(memory_space=pltpu.VMEM)

    def call(*args):
        specs = [pl.BlockSpec(memory_space=pltpu.SMEM)] * scalars
        specs += [pl.BlockSpec(memory_space=pltpu.HBM)] * far
        specs += [whole] * (len(args) - scalars - far)
        return pl.pallas_call(
            body,
            out_shape=out_shape,
            in_specs=specs,
            out_specs=jax.tree.map(lambda _: whole, out_shape),
            scratch_shapes=list(scratch),
            compiler_params=pltpu.CompilerParams(vmem_limit_bytes=limit * MIB),
        )(*args)

    return call


def shape(dims, dtype=F32):
    return jax.ShapeDtypeStruct(dims, dtype)


def picked_unit(patches, positions):
    patch = lax.broadcasted_iota(jnp.int32, (patches.shape[0], positions.shape[1]), 0)
    onehot = (patch == positions).astype(F32).astype(BF16)
    rows = lax.dot_general(
        onehot, patches, (((0,), (0,)), ((), ())), preferred_element_type=F32
    )
    inverse = lax.rsqrt(jnp.sum(rows * rows, axis=1, keepdims=True) + EPSILON)
    return rows * inverse, inverse


def far_off(array):
    return pltpu.with_memory_space_constraint(array, pltpu.HBM)


def lane_tiles(row, count):
    return jnp.concatenate(
        [jnp.broadcast_to(row[i : i + 1, :], (8, LANES)) for i in range(count)], axis=1
    )


def column(row):
    return jnp.transpose(jnp.broadcast_to(row, (LANES, LANES)))


def fold(block):
    tiles = [block[:, i : i + LANES] for i in range(0, block.shape[1], LANES)]
    while len(tiles) > 1:
        tiles = [a + b for a, b in zip(tiles[::2], tiles[1::2])]
    return tiles[0]


def row_sums(partial):
    total = lax.dot_general(
        jnp.ones((8, LANES), F32),
        partial,
        (((1,), (1,)), ((), ())),
        precision=lax.Precision.HIGHEST,
        preferred_element_type=F32,
    )
    return jnp.concatenate(
        [total[0:1, i : i + LANES] for i in range(0, partial.shape[0], LANES)], axis=0
    )


def col_tiles(total):
    return jnp.concatenate(
        [total[:, i : i + LANES] for i in range(0, total.shape[1], LANES)], axis=0
    )


def start_kernel(
    weight_hbm, teacher_hbm, student_hbm, index_hbm,
    back_ref, inv_ref, teacher_exp_ref, msg_ref,
    own_unit_ref, own_inv_ref, flip_ref, logits_ref, student_exp_ref, part_ref,
    weight_ref, teacher_ref, student_ref, index_ref, norm_ref, teacher_norm_ref, unit_ref, row_inv_ref,
    tail, sems,
):
    copies = [
        pltpu.make_async_copy(source, target, sems.at[i])
        for i, (source, target) in enumerate(
            [
                (index_hbm, index_ref),
                (teacher_hbm, teacher_ref),
                (weight_hbm, weight_ref),
                (student_hbm, student_ref),
            ]
        )
    ]
    for copy in copies:
        copy.start()
    copies[0].wait()
    copies[1].wait()
    for view in range(teacher_ref.shape[0]):
        unit, _ = picked_unit(teacher_ref[view], index_ref[view : view + 1, :])
        teacher_norm_ref[view * LANES : (view + 1) * LANES, :] = unit.astype(BF16)
    copies[2].wait()
    wide = weight_ref[...].astype(F32)
    inverse = lax.rsqrt(jnp.sum(wide * wide, axis=0, keepdims=True) + EPSILON)
    inv_ref[...] = inverse
    norm_ref[...] = (wide * inverse).astype(BF16)
    back_ref[...] = jnp.transpose(norm_ref[...])
    total = jnp.zeros((1, weight_ref.shape[1]), F32)
    for view in range(teacher_ref.shape[0]):
        rows = slice(view * LANES, (view + 1) * LANES)
        logits = jnp.dot(teacher_norm_ref[rows, :], norm_ref[...], preferred_element_type=F32)
        block = jnp.exp2(logits * (LOG2_E / TEACHER_TEMP))
        teacher_exp_ref[rows, :] = block
        total += jnp.sum(block, axis=0, keepdims=True)
    msg_ref[...] = col_tiles(total)
    copies[3].wait()
    for view in range(student_ref.shape[0]):
        rows = slice(view * LANES, (view + 1) * LANES)
        unit, inverse = picked_unit(student_ref[view], index_ref[view : view + 1, :])
        unit_ref[rows, :] = unit
        row_inv_ref[rows, :] = jnp.broadcast_to(inverse, (LANES, LANES))
        narrow = unit.astype(BF16)
        flip_ref[:, rows] = jnp.transpose(narrow)
        logits = jnp.dot(narrow, norm_ref[...], preferred_element_type=F32)
        block = jnp.exp2(logits * (LOG2_E / STUDENT_TEMP))
        logits_ref[rows, :] = logits
        student_exp_ref[rows, :] = block
        tail[rows, :] = fold(block)
    part_ref[...] = row_sums(tail[...])
    head_index = lax.axis_index("head")
    first = (head_index & 3) * LANES + (head_index >> 2) * own_unit_ref.shape[0]
    own = pl.ds(pl.multiple_of(first, 16), own_unit_ref.shape[0])
    own_unit_ref[...] = unit_ref[own, :]
    own_inv_ref[...] = row_inv_ref[own, :]


def row_kernel(has_extra, *refs):
    if has_extra:
        cols_ref, exp_ref, extra_ref, msg_ref, tail = refs
    else:
        cols_ref, exp_ref, msg_ref, tail = refs
    scale = lane_tiles(1.0 / jnp.sum(cols_ref[...], axis=0), cols_ref.shape[1])

    def step(i, carry):
        start = pl.multiple_of(i * 8, 8)
        tail[pl.ds(start, 8), :] = fold(exp_ref[pl.ds(start, 8), :] * scale)
        return carry

    lax.fori_loop(0, exp_ref.shape[0] // 8, step, 0, unroll=8)
    out = row_sums(tail[...])
    if has_extra:
        out = jnp.concatenate([out, extra_ref[...]], axis=0)
    msg_ref[...] = jnp.broadcast_to(out[None], msg_ref.shape)


def col_kernel(has_extra, rows_ref, exp_ref, *refs):
    if has_extra:
        msg_ref, extra_ref, scale_ref = refs
    else:
        msg_ref, scale_ref = refs
    total = jnp.sum(rows_ref[...], axis=0)
    if has_extra:
        extra_ref[...] = total[4:8, :]
    scale = 1.0 / total[0:4, :]
    for j in range(4):
        scale_ref[j * LANES : (j + 1) * LANES, :] = column(scale[j : j + 1, :])
    count = exp_ref.shape[1] // LANES

    def step(i, sums):
        start = pl.multiple_of(i * 8, 8)
        factor = scale_ref[pl.ds(start, 8), :]
        return tuple(
            sums[k] + exp_ref[pl.ds(start, 8), k * LANES : (k + 1) * LANES] * factor
            for k in range(count)
        )

    sums = lax.fori_loop(
        0, exp_ref.shape[0] // 8, step, (jnp.zeros((8, LANES), F32),) * count, unroll=8
    )
    msg_ref[...] = jnp.concatenate([jnp.sum(s, axis=0, keepdims=True) for s in sums], axis=0)


def last_row_kernel(cols_ref, exp_ref, logits_ref, msg_ref, scale_ref, tail, weighted):
    small = 1.0 / jnp.sum(cols_ref[...], axis=0)
    scale = lane_tiles(small, cols_ref.shape[1])
    scale_ref[...] = scale

    def step(i, carry):
        start = pl.multiple_of(i * 8, 8)
        scaled = exp_ref[pl.ds(start, 8), :] * scale
        tail[pl.ds(start, 8), :] = fold(scaled)
        weighted[pl.ds(start, 8), :] = fold(scaled * logits_ref[pl.ds(start, 8), :])
        return carry

    lax.fori_loop(0, exp_ref.shape[0] // 8, step, 0, unroll=4)
    out = jnp.concatenate([row_sums(tail[...]), row_sums(weighted[...])], axis=0)
    msg_ref[...] = jnp.broadcast_to(out[None], msg_ref.shape)


def grad_kernel(
    rows_ref, partition_ref, scale_ref, exp_ref, student_ref, flip_ref, back_ref,
    weight_ref, inv_ref, keep_ref, send_ref, pull_ref, factor, softener, logits,
):
    total = jnp.sum(rows_ref[...], axis=0)
    partition = partition_ref[...]
    scale = 1.0 / total[0:4, :]
    losses = jnp.log(partition) - scale * total[4:8, :] * (1.0 / STUDENT_TEMP)
    loss = jnp.sum(jnp.sum(losses, axis=1, keepdims=True), axis=0, keepdims=True)
    columns = exp_ref.shape[1]
    for ref in (keep_ref, send_ref):
        ref[:, :, :, columns:] = jnp.broadcast_to(loss[None, None], ref.shape[:3] + (LANES,))
    softener_rows = 1.0 / partition
    for j in range(4):
        rows = slice(j * LANES, (j + 1) * LANES)
        factor[rows, :] = column(scale[j : j + 1, :])
        softener[rows, :] = column(softener_rows[j : j + 1, :])
    width = logits.shape[1]
    batch_index = lax.axis_index("batch")
    core, x_index, z_high = batch_index & 1, batch_index >> 2, (batch_index >> 1) & 1
    wide = (LANES, width)
    for block in range(columns // width):
        cols = slice(block * width, (block + 1) * width)
        for j in range(4):
            rows = slice(j * LANES, (j + 1) * LANES)
            soft = jnp.concatenate([softener[rows, :]] * (width // LANES), axis=1)
            hard = jnp.concatenate([factor[rows, :]] * (width // LANES), axis=1)
            targets = hard * (exp_ref[rows, cols] * scale_ref[0:1, cols])
            logits[rows, :] = (
                (student_ref[rows, cols] * soft - targets) * (1.0 / STUDENT_TEMP)
            ).astype(BF16)
        pull = jnp.dot(logits[...], back_ref[cols, :], preferred_element_type=F32)
        pull = pull.reshape(pull_ref.shape)
        pull_ref[...] = pull if block == 0 else pull_ref[...] + pull
        unit = jnp.dot(flip_ref[...], logits[...], preferred_element_type=F32)
        inverse = inv_ref[:, cols]
        weight_unit = weight_ref[:, cols].astype(F32) * inverse
        inner = jnp.sum(weight_unit * unit, axis=0, keepdims=True)
        full = (inverse * (unit - weight_unit * inner)).reshape(4, 2, 2, 16, width)
        first, second = full[:, :, 0], full[:, :, 1]
        for x in range(4):
            for z in range(2):
                place = ((x - x_index) & 3, z ^ z_high)
                keep_ref[place + (slice(None), cols)] = jnp.where(
                    core == 0, first[x, z], second[x, z]
                )
                send_ref[place + (slice(None), cols)] = jnp.where(
                    core == 0, second[x, z], first[x, z]
                )


def pair_kernel(pair_ref, copies_ref):
    copies_ref[...] = jnp.broadcast_to(jnp.sum(pair_ref[...], axis=0)[None], copies_ref.shape)


def finish_kernel(blocks_ref, unit_ref, inv_ref, copies_ref):
    pull = jnp.sum(blocks_ref[...], axis=0)
    unit = unit_ref[...]
    inner = jnp.sum(unit * pull, axis=1, keepdims=True)
    rows = inv_ref[:, 0:1] * (pull - unit * inner)
    copies_ref[...] = jnp.broadcast_to(rows[None], copies_ref.shape)


def exchange(blocks, axis, groups=None):
    return lax.all_to_all(blocks, axis, 0, 0, axis_index_groups=groups)


def share(block, axis, groups, count):
    return exchange(jnp.broadcast_to(block[None], (count,) + block.shape), axis, groups)


def over_batch(block):
    pairs = [[i, i + 1] for i in range(0, 16, 2)]
    rest = [[i for i in range(16) if i % 2 == core] for core in range(2)]
    both = lax.all_gather(block, "batch", axis_index_groups=pairs)
    copies = kernel_call(pair_kernel, shape((8,) + block.shape), limit=4)(both)
    return exchange(copies, "batch", rest)


def tie(*values):
    return lax.optimization_barrier(values)


def per_device(student_patches, teacher_patches, mask_index, weight):
    view_count, masked_count = mask_index.shape
    feature_dim, columns = weight.shape
    total = view_count * masked_count
    share_rows = feature_dim // 16
    y_groups = [[4 * z + y for y in range(4)] for z in range(8)]
    z_groups = [[4 * z + y for z in range(8)] for y in range(4)]
    col_msg = shape((columns // LANES, LANES))
    row_msg = shape((32, total // LANES, LANES))
    row_msg_two = shape((32, 2 * total // LANES, LANES))
    tail = pltpu.VMEM((total, LANES), F32)

    (
        back, weight_inv, teacher_exp, cols,
        unit, inverse, flip, logits, student_exp, partition_part,
    ) = kernel_call(
        start_kernel,
        (
            shape((columns, feature_dim), BF16),
            shape((1, columns)),
            shape((total, columns)),
            col_msg,
            shape((total // 32, feature_dim)),
            shape((total // 32, LANES)),
            shape((feature_dim, total), BF16),
            shape((total, columns)),
            shape((total, columns)),
            shape((total // LANES, LANES)),
        ),
        [
            pltpu.VMEM(weight.shape, BF16),
            pltpu.VMEM(teacher_patches.shape, BF16),
            pltpu.VMEM(student_patches.shape, BF16),
            pltpu.VMEM(mask_index.shape, jnp.int32),
            pltpu.VMEM((feature_dim, columns), BF16),
            pltpu.VMEM((total, feature_dim), BF16),
            pltpu.VMEM((total, feature_dim), F32),
            tail,
            tail,
            pltpu.SemaphoreType.DMA((4,)),
        ],
        far=4,
        limit=16,
    )(
        far_off(weight), far_off(teacher_patches), far_off(student_patches),
        far_off(mask_index),
    )
    cols = over_batch(cols)
    rows = kernel_call(functools.partial(row_kernel, True), row_msg_two, [tail])(
        cols, teacher_exp, partition_part
    )
    rows = exchange(rows, "head")
    cols, partition = kernel_call(
        functools.partial(col_kernel, True), (col_msg, shape((total // LANES, LANES))), [tail]
    )(rows, teacher_exp)
    cols = over_batch(cols)
    rows = kernel_call(functools.partial(row_kernel, False), row_msg, [tail])(cols, teacher_exp)
    rows = exchange(rows, "head")
    cols = kernel_call(functools.partial(col_kernel, False), col_msg, [tail])(rows, teacher_exp)
    cols = over_batch(cols)
    rows, col_scale = kernel_call(
        last_row_kernel, (row_msg_two, shape((8, columns))), [tail, tail]
    )(cols, teacher_exp, logits)
    rows = exchange(rows, "head")

    part = shape((4, 2, share_rows, columns + LANES))
    keep, send, pull = kernel_call(
        grad_kernel,
        (part, part, shape((4, total // 4, feature_dim))),
        [tail, tail, pltpu.VMEM((total, 512), BF16)],
        limit=16,
    )(
        rows, partition, col_scale, teacher_exp, student_exp, flip, back, weight,
        weight_inv,
    )
    parts = keep + lax.ppermute(send, "batch", [(i, i ^ 1) for i in range(16)])
    parts, pull = tie(parts, pull)
    piece = jnp.sum(exchange(pull, "head", y_groups), axis=0)

    held = parts[0]
    for step in (1, 2, 3):
        pairs = [(i, (i + 4 * step) % 16) for i in range(16)]
        held = held + lax.ppermute(parts[step], "batch", pairs)

    piece = kernel_call(finish_kernel, shape((8, total // 32, feature_dim)))(
        exchange(piece.reshape(8, total // 32, feature_dim), "head", z_groups), unit, inverse
    )
    piece = exchange(piece, "head", z_groups).reshape(total // 4, feature_dim)
    grad_weight = held[0] + lax.ppermute(held[1], "batch", [(i, i ^ 2) for i in range(16)])
    grad_rows = share(piece, "head", y_groups, 4).reshape(view_count, masked_count, feature_dim)
    loss = grad_weight[0, columns] / (total * lax.axis_size("batch"))
    return (grad_rows, grad_weight[:, :columns], loss)


def solution(mesh):
    in_specs = (P("batch", None, None), P("batch", None, None), P("batch", None), P(None, "head"))
    out_specs = (P("batch", None, None), P("batch", "head"), P())
    return jax.shard_map(
        per_device, mesh=mesh, in_specs=in_specs, out_specs=out_specs, check_vma=False
    )
```

```python
import functools

import jax
import jax.numpy as jnp
from jax import lax
from jax.experimental import pallas as pl
from jax.experimental.pallas import tpu as pltpu
from jax.sharding import PartitionSpec as P

TEACHER_TEMP = 0.07
STUDENT_TEMP = 0.1
EPSILON = 1e-06
LOG2_E = 1.4426950408889634
LANES = 128
F32 = jnp.float32
BF16 = jnp.bfloat16
MIB = 1 << 20


def kernel_call(body, out_shape, scratch=(), limit=12, scalars=0, far=0):
    whole = pl.BlockSpec(memory_space=pltpu.VMEM)

    def call(*args):
        specs = [pl.BlockSpec(memory_space=pltpu.SMEM)] * scalars
        specs += [pl.BlockSpec(memory_space=pltpu.HBM)] * far
        specs += [whole] * (len(args) - scalars - far)
        return pl.pallas_call(
            body,
            out_shape=out_shape,
            in_specs=specs,
            out_specs=jax.tree.map(lambda _: whole, out_shape),
            scratch_shapes=list(scratch),
            compiler_params=pltpu.CompilerParams(vmem_limit_bytes=limit * MIB),
        )(*args)

    return call


def shape(dims, dtype=F32):
    return jax.ShapeDtypeStruct(dims, dtype)


def picked_unit(patches, positions):
    patch = lax.broadcasted_iota(jnp.int32, (patches.shape[0], positions.shape[1]), 0)
    onehot = (patch == positions).astype(F32).astype(BF16)
    rows = lax.dot_general(
        onehot, patches, (((0,), (0,)), ((), ())), preferred_element_type=F32
    )
    inverse = lax.rsqrt(jnp.sum(rows * rows, axis=1, keepdims=True) + EPSILON)
    return rows * inverse, inverse


def far_off(array):
    return pltpu.with_memory_space_constraint(array, pltpu.HBM)


def lane_tiles(row, count):
    return jnp.concatenate(
        [jnp.broadcast_to(row[i : i + 1, :], (8, LANES)) for i in range(count)], axis=1
    )


def column(row):
    return jnp.transpose(jnp.broadcast_to(row, (LANES, LANES)))


def fold(block):
    tiles = [block[:, i : i + LANES] for i in range(0, block.shape[1], LANES)]
    while len(tiles) > 1:
        tiles = [a + b for a, b in zip(tiles[::2], tiles[1::2])]
    return tiles[0]


def row_sums(partial):
    total = lax.dot_general(
        jnp.ones((8, LANES), F32),
        partial,
        (((1,), (1,)), ((), ())),
        precision=lax.Precision.HIGHEST,
        preferred_element_type=F32,
    )
    return jnp.concatenate(
        [total[0:1, i : i + LANES] for i in range(0, partial.shape[0], LANES)], axis=0
    )


def col_tiles(total):
    return jnp.concatenate(
        [total[:, i : i + LANES] for i in range(0, total.shape[1], LANES)], axis=0
    )


def start_kernel(
    weight_hbm, teacher_hbm, student_hbm, index_hbm,
    back_ref, inv_ref, teacher_exp_ref, msg_ref,
    own_unit_ref, own_inv_ref, flip_ref, logits_ref, student_exp_ref, part_ref,
    weight_ref, teacher_ref, student_ref, index_ref, norm_ref, teacher_norm_ref, unit_ref, row_inv_ref,
    tail, sems,
):
    copies = [
        pltpu.make_async_copy(source, target, sems.at[i])
        for i, (source, target) in enumerate(
            [
                (index_hbm, index_ref),
                (teacher_hbm, teacher_ref),
                (weight_hbm, weight_ref),
                (student_hbm, student_ref),
            ]
        )
    ]
    for copy in copies:
        copy.start()
    copies[0].wait()
    copies[1].wait()
    for view in range(teacher_ref.shape[0]):
        unit, _ = picked_unit(teacher_ref[view], index_ref[view : view + 1, :])
        teacher_norm_ref[view * LANES : (view + 1) * LANES, :] = unit.astype(BF16)
    copies[2].wait()
    wide = weight_ref[...].astype(F32)
    inverse = lax.rsqrt(jnp.sum(wide * wide, axis=0, keepdims=True) + EPSILON)
    inv_ref[...] = inverse
    norm_ref[...] = (wide * inverse).astype(BF16)
    back_ref[...] = jnp.transpose(norm_ref[...])
    total = jnp.zeros((1, weight_ref.shape[1]), F32)
    for view in range(teacher_ref.shape[0]):
        rows = slice(view * LANES, (view + 1) * LANES)
        logits = jnp.dot(teacher_norm_ref[rows, :], norm_ref[...], preferred_element_type=F32)
        block = jnp.exp2(logits * (LOG2_E / TEACHER_TEMP))
        teacher_exp_ref[rows, :] = block
        total += jnp.sum(block, axis=0, keepdims=True)
    msg_ref[...] = col_tiles(total)
    copies[3].wait()
    for view in range(student_ref.shape[0]):
        rows = slice(view * LANES, (view + 1) * LANES)
        unit, inverse = picked_unit(student_ref[view], index_ref[view : view + 1, :])
        unit_ref[rows, :] = unit
        row_inv_ref[rows, :] = jnp.broadcast_to(inverse, (LANES, LANES))
        narrow = unit.astype(BF16)
        flip_ref[:, rows] = jnp.transpose(narrow)
        logits = jnp.dot(narrow, norm_ref[...], preferred_element_type=F32)
        block = jnp.exp2(logits * (LOG2_E / STUDENT_TEMP))
        logits_ref[rows, :] = logits
        student_exp_ref[rows, :] = block
        tail[rows, :] = fold(block)
    part_ref[...] = row_sums(tail[...])
    head_index = lax.axis_index("head")
    first = (head_index & 3) * LANES + (head_index >> 2) * own_unit_ref.shape[0]
    own = pl.ds(pl.multiple_of(first, 16), own_unit_ref.shape[0])
    own_unit_ref[...] = unit_ref[own, :]
    own_inv_ref[...] = row_inv_ref[own, :]


def row_kernel(has_extra, *refs):
    if has_extra:
        cols_ref, exp_ref, extra_ref, msg_ref, tail = refs
    else:
        cols_ref, exp_ref, msg_ref, tail = refs
    scale = lane_tiles(1.0 / jnp.sum(cols_ref[...], axis=0), cols_ref.shape[1])

    def step(i, carry):
        start = pl.multiple_of(i * 8, 8)
        tail[pl.ds(start, 8), :] = fold(exp_ref[pl.ds(start, 8), :] * scale)
        return carry

    lax.fori_loop(0, exp_ref.shape[0] // 8, step, 0, unroll=8)
    out = row_sums(tail[...])
    if has_extra:
        out = jnp.concatenate([out, extra_ref[...]], axis=0)
    msg_ref[...] = jnp.broadcast_to(out[None], msg_ref.shape)


def col_kernel(has_extra, rows_ref, exp_ref, *refs):
    if has_extra:
        msg_ref, extra_ref, scale_ref = refs
    else:
        msg_ref, scale_ref = refs
    total = jnp.sum(rows_ref[...], axis=0)
    if has_extra:
        extra_ref[...] = total[4:8, :]
    scale = 1.0 / total[0:4, :]
    for j in range(4):
        scale_ref[j * LANES : (j + 1) * LANES, :] = column(scale[j : j + 1, :])
    count = exp_ref.shape[1] // LANES

    def step(i, sums):
        start = pl.multiple_of(i * 8, 8)
        factor = scale_ref[pl.ds(start, 8), :]
        return tuple(
            sums[k] + exp_ref[pl.ds(start, 8), k * LANES : (k + 1) * LANES] * factor
            for k in range(count)
        )

    sums = lax.fori_loop(
        0, exp_ref.shape[0] // 8, step, (jnp.zeros((8, LANES), F32),) * count, unroll=8
    )
    msg_ref[...] = jnp.concatenate([jnp.sum(s, axis=0, keepdims=True) for s in sums], axis=0)


def last_row_kernel(cols_ref, exp_ref, logits_ref, msg_ref, scale_ref, tail, weighted):
    small = 1.0 / jnp.sum(cols_ref[...], axis=0)
    scale = lane_tiles(small, cols_ref.shape[1])
    scale_ref[...] = scale

    def step(i, carry):
        start = pl.multiple_of(i * 8, 8)
        scaled = exp_ref[pl.ds(start, 8), :] * scale
        tail[pl.ds(start, 8), :] = fold(scaled)
        weighted[pl.ds(start, 8), :] = fold(scaled * logits_ref[pl.ds(start, 8), :])
        return carry

    lax.fori_loop(0, exp_ref.shape[0] // 8, step, 0, unroll=4)
    out = jnp.concatenate([row_sums(tail[...]), row_sums(weighted[...])], axis=0)
    msg_ref[...] = jnp.broadcast_to(out[None], msg_ref.shape)


def grad_kernel(
    rows_ref, partition_ref, scale_ref, exp_ref, student_ref, back_ref,
    logits_ref, pull_ref, loss_ref, factor, softener,
):
    total = jnp.sum(rows_ref[...], axis=0)
    partition = partition_ref[...]
    scale = 1.0 / total[0:4, :]
    losses = jnp.log(partition) - scale * total[4:8, :] * (1.0 / STUDENT_TEMP)
    loss = jnp.sum(jnp.sum(losses, axis=1, keepdims=True), axis=0, keepdims=True)
    loss_ref[...] = jnp.broadcast_to(loss, loss_ref.shape)
    softener_rows = 1.0 / partition
    for j in range(4):
        rows = slice(j * LANES, (j + 1) * LANES)
        factor[rows, :] = column(scale[j : j + 1, :])
        softener[rows, :] = column(softener_rows[j : j + 1, :])
    width = 512
    for block in range(exp_ref.shape[1] // width):
        cols = slice(block * width, (block + 1) * width)
        for j in range(4):
            rows = slice(j * LANES, (j + 1) * LANES)
            soft = jnp.concatenate([softener[rows, :]] * (width // LANES), axis=1)
            hard = jnp.concatenate([factor[rows, :]] * (width // LANES), axis=1)
            targets = hard * (exp_ref[rows, cols] * scale_ref[0:1, cols])
            logits_ref[rows, cols] = (
                (student_ref[rows, cols] * soft - targets) * (1.0 / STUDENT_TEMP)
            ).astype(BF16)
        pull = jnp.dot(logits_ref[:, cols], back_ref[cols, :], preferred_element_type=F32)
        pull = pull.reshape(pull_ref.shape)
        pull_ref[...] = pull if block == 0 else pull_ref[...] + pull


def unit_kernel(logits_ref, loss_ref, flip_ref, weight_ref, inv_ref, keep_ref, send_ref):
    columns = weight_ref.shape[1]
    for ref in (keep_ref, send_ref):
        ref[:, :, :, columns:] = jnp.broadcast_to(
            loss_ref[0:1, :][None, None], ref.shape[:3] + (LANES,)
        )
    batch_index = lax.axis_index("batch")
    core, x_index, z_high = batch_index & 1, batch_index >> 2, (batch_index >> 1) & 1
    width = 512
    for block in range(columns // width):
        cols = slice(block * width, (block + 1) * width)
        unit = jnp.dot(flip_ref[...], logits_ref[:, cols], preferred_element_type=F32)
        inverse = inv_ref[:, cols]
        weight_unit = weight_ref[:, cols].astype(F32) * inverse
        inner = jnp.sum(weight_unit * unit, axis=0, keepdims=True)
        full = (inverse * (unit - weight_unit * inner)).reshape(4, 2, 2, 16, width)
        first, second = full[:, :, 0], full[:, :, 1]
        for x in range(4):
            for z in range(2):
                place = ((x - x_index) & 3, z ^ z_high)
                keep_ref[place + (slice(None), cols)] = jnp.where(
                    core == 0, first[x, z], second[x, z]
                )
                send_ref[place + (slice(None), cols)] = jnp.where(
                    core == 0, second[x, z], first[x, z]
                )


def pair_kernel(pair_ref, copies_ref):
    copies_ref[...] = jnp.broadcast_to(jnp.sum(pair_ref[...], axis=0)[None], copies_ref.shape)


def finish_kernel(blocks_ref, unit_ref, inv_ref, copies_ref):
    pull = jnp.sum(blocks_ref[...], axis=0)
    unit = unit_ref[...]
    inner = jnp.sum(unit * pull, axis=1, keepdims=True)
    rows = inv_ref[:, 0:1] * (pull - unit * inner)
    copies_ref[...] = jnp.broadcast_to(rows[None], copies_ref.shape)


def exchange(blocks, axis, groups=None):
    return lax.all_to_all(blocks, axis, 0, 0, axis_index_groups=groups)


def share(block, axis, groups, count):
    return exchange(jnp.broadcast_to(block[None], (count,) + block.shape), axis, groups)


def over_batch(block):
    pairs = [[i, i + 1] for i in range(0, 16, 2)]
    rest = [[i for i in range(16) if i % 2 == core] for core in range(2)]
    both = lax.all_gather(block, "batch", axis_index_groups=pairs)
    copies = kernel_call(pair_kernel, shape((8,) + block.shape), limit=4)(both)
    return exchange(copies, "batch", rest)


def tie(*values):
    return lax.optimization_barrier(values)


def per_device(student_patches, teacher_patches, mask_index, weight):
    view_count, masked_count = mask_index.shape
    feature_dim, columns = weight.shape
    total = view_count * masked_count
    share_rows = feature_dim // 16
    y_groups = [[4 * z + y for y in range(4)] for z in range(8)]
    z_groups = [[4 * z + y for z in range(8)] for y in range(4)]
    col_msg = shape((columns // LANES, LANES))
    row_msg = shape((32, total // LANES, LANES))
    row_msg_two = shape((32, 2 * total // LANES, LANES))
    tail = pltpu.VMEM((total, LANES), F32)

    (
        back, weight_inv, teacher_exp, cols,
        unit, inverse, flip, logits, student_exp, partition_part,
    ) = kernel_call(
        start_kernel,
        (
            shape((columns, feature_dim), BF16),
            shape((1, columns)),
            shape((total, columns)),
            col_msg,
            shape((total // 32, feature_dim)),
            shape((total // 32, LANES)),
            shape((feature_dim, total), BF16),
            shape((total, columns)),
            shape((total, columns)),
            shape((total // LANES, LANES)),
        ),
        [
            pltpu.VMEM(weight.shape, BF16),
            pltpu.VMEM(teacher_patches.shape, BF16),
            pltpu.VMEM(student_patches.shape, BF16),
            pltpu.VMEM(mask_index.shape, jnp.int32),
            pltpu.VMEM((feature_dim, columns), BF16),
            pltpu.VMEM((total, feature_dim), BF16),
            pltpu.VMEM((total, feature_dim), F32),
            tail,
            tail,
            pltpu.SemaphoreType.DMA((4,)),
        ],
        far=4,
        limit=16,
    )(
        far_off(weight), far_off(teacher_patches), far_off(student_patches),
        far_off(mask_index),
    )
    cols = over_batch(cols)
    rows = kernel_call(functools.partial(row_kernel, True), row_msg_two, [tail])(
        cols, teacher_exp, partition_part
    )
    rows = exchange(rows, "head")
    cols, partition = kernel_call(
        functools.partial(col_kernel, True), (col_msg, shape((total // LANES, LANES))), [tail]
    )(rows, teacher_exp)
    cols = over_batch(cols)
    rows = kernel_call(functools.partial(row_kernel, False), row_msg, [tail])(cols, teacher_exp)
    rows = exchange(rows, "head")
    cols = kernel_call(functools.partial(col_kernel, False), col_msg, [tail])(rows, teacher_exp)
    cols = over_batch(cols)
    rows, col_scale = kernel_call(
        last_row_kernel, (row_msg_two, shape((8, columns))), [tail, tail]
    )(cols, teacher_exp, logits)
    rows = exchange(rows, "head")

    part = shape((4, 2, share_rows, columns + LANES))
    grad_logits, pull, loss_part = kernel_call(
        grad_kernel,
        (
            shape((total, columns), BF16),
            shape((4, total // 4, feature_dim)),
            shape((8, LANES)),
        ),
        [tail, tail],
    )(rows, partition, col_scale, teacher_exp, student_exp, back)
    keep, send = kernel_call(unit_kernel, (part, part))(
        grad_logits, loss_part, flip, weight, weight_inv
    )
    parts = keep + lax.ppermute(send, "batch", [(i, i ^ 1) for i in range(16)])
    parts, pull = tie(parts, pull)
    piece = jnp.sum(exchange(pull, "head", y_groups), axis=0)

    held = parts[0]
    for step in (1, 2, 3):
        pairs = [(i, (i + 4 * step) % 16) for i in range(16)]
        held = held + lax.ppermute(parts[step], "batch", pairs)

    piece = kernel_call(finish_kernel, shape((8, total // 32, feature_dim)))(
        exchange(piece.reshape(8, total // 32, feature_dim), "head", z_groups), unit, inverse
    )
    piece = exchange(piece, "head", z_groups).reshape(total // 4, feature_dim)
    grad_weight = held[0] + lax.ppermute(held[1], "batch", [(i, i ^ 2) for i in range(16)])
    grad_rows = share(piece, "head", y_groups, 4).reshape(view_count, masked_count, feature_dim)
    loss = grad_weight[0, columns] / (total * lax.axis_size("batch"))
    return (grad_rows, grad_weight[:, :columns], loss)


def solution(mesh):
    in_specs = (P("batch", None, None), P("batch", None, None), P("batch", None), P(None, "head"))
    out_specs = (P("batch", None, None), P("batch", "head"), P())
    return jax.shard_map(
        per_device, mesh=mesh, in_specs=in_specs, out_specs=out_specs, check_vma=False
    )
```

```python
import functools

import jax
import jax.numpy as jnp
from jax import lax
from jax.experimental import pallas as pl
from jax.experimental.pallas import tpu as pltpu
from jax.sharding import PartitionSpec as P

TEACHER_TEMP = 0.07
STUDENT_TEMP = 0.1
EPSILON = 1e-06
LOG2_E = 1.4426950408889634
LANES = 128
F32 = jnp.float32
BF16 = jnp.bfloat16
MIB = 1 << 20


def kernel_call(body, out_shape, scratch=(), limit=12, scalars=0, far=0):
    whole = pl.BlockSpec(memory_space=pltpu.VMEM)

    def call(*args):
        specs = [pl.BlockSpec(memory_space=pltpu.SMEM)] * scalars
        specs += [pl.BlockSpec(memory_space=pltpu.HBM)] * far
        specs += [whole] * (len(args) - scalars - far)
        return pl.pallas_call(
            body,
            out_shape=out_shape,
            in_specs=specs,
            out_specs=jax.tree.map(lambda _: whole, out_shape),
            scratch_shapes=list(scratch),
            compiler_params=pltpu.CompilerParams(vmem_limit_bytes=limit * MIB),
        )(*args)

    return call


def shape(dims, dtype=F32):
    return jax.ShapeDtypeStruct(dims, dtype)


def picked_unit(patches, positions):
    patch = lax.broadcasted_iota(jnp.int32, (patches.shape[0], positions.shape[1]), 0)
    onehot = (patch == positions).astype(F32).astype(BF16)
    rows = lax.dot_general(
        onehot, patches, (((0,), (0,)), ((), ())), preferred_element_type=F32
    )
    inverse = lax.rsqrt(jnp.sum(rows * rows, axis=1, keepdims=True) + EPSILON)
    return rows * inverse, inverse


def far_off(array):
    return pltpu.with_memory_space_constraint(array, pltpu.HBM)


def lane_tiles(row, count):
    return jnp.concatenate(
        [jnp.broadcast_to(row[i : i + 1, :], (8, LANES)) for i in range(count)], axis=1
    )


def column(row):
    return jnp.transpose(jnp.broadcast_to(row, (LANES, LANES)))


def fold(block):
    tiles = [block[:, i : i + LANES] for i in range(0, block.shape[1], LANES)]
    while len(tiles) > 1:
        tiles = [a + b for a, b in zip(tiles[::2], tiles[1::2])]
    return tiles[0]


def row_sums(partial):
    total = lax.dot_general(
        jnp.ones((8, LANES), F32),
        partial,
        (((1,), (1,)), ((), ())),
        precision=lax.Precision.HIGHEST,
        preferred_element_type=F32,
    )
    return jnp.concatenate(
        [total[0:1, i : i + LANES] for i in range(0, partial.shape[0], LANES)], axis=0
    )


def col_tiles(total):
    return jnp.concatenate(
        [total[:, i : i + LANES] for i in range(0, total.shape[1], LANES)], axis=0
    )


def start_kernel(
    weight_hbm, teacher_hbm, student_hbm, index_hbm,
    back_ref, inv_ref, teacher_exp_ref, msg_ref,
    own_unit_ref, own_inv_ref, flip_ref, logits_ref, student_exp_ref, part_ref,
    weight_ref, teacher_ref, student_ref, index_ref, norm_ref, teacher_norm_ref, unit_ref, row_inv_ref,
    tail, sems,
):
    copies = [
        pltpu.make_async_copy(source, target, sems.at[i])
        for i, (source, target) in enumerate(
            [
                (index_hbm, index_ref),
                (teacher_hbm, teacher_ref),
                (weight_hbm, weight_ref),
                (student_hbm, student_ref),
            ]
        )
    ]
    for copy in copies:
        copy.start()
    copies[0].wait()
    copies[1].wait()
    for view in range(teacher_ref.shape[0]):
        unit, _ = picked_unit(teacher_ref[view], index_ref[view : view + 1, :])
        teacher_norm_ref[view * LANES : (view + 1) * LANES, :] = unit.astype(BF16)
    copies[2].wait()
    wide = weight_ref[...].astype(F32)
    inverse = lax.rsqrt(jnp.sum(wide * wide, axis=0, keepdims=True) + EPSILON)
    inv_ref[...] = inverse
    norm_ref[...] = (wide * inverse).astype(BF16)
    back_ref[...] = jnp.transpose(norm_ref[...])
    total = jnp.zeros((1, weight_ref.shape[1]), F32)
    for view in range(teacher_ref.shape[0]):
        rows = slice(view * LANES, (view + 1) * LANES)
        logits = jnp.dot(teacher_norm_ref[rows, :], norm_ref[...], preferred_element_type=F32)
        block = jnp.exp2(logits * (LOG2_E / TEACHER_TEMP))
        teacher_exp_ref[rows, :] = block
        total += jnp.sum(block, axis=0, keepdims=True)
    msg_ref[...] = col_tiles(total)
    copies[3].wait()
    for view in range(student_ref.shape[0]):
        rows = slice(view * LANES, (view + 1) * LANES)
        unit, inverse = picked_unit(student_ref[view], index_ref[view : view + 1, :])
        unit_ref[rows, :] = unit
        row_inv_ref[rows, :] = jnp.broadcast_to(inverse, (LANES, LANES))
        narrow = unit.astype(BF16)
        flip_ref[:, rows] = jnp.transpose(narrow)
        logits = jnp.dot(narrow, norm_ref[...], preferred_element_type=F32)
        block = jnp.exp2(logits * (LOG2_E / STUDENT_TEMP))
        logits_ref[rows, :] = logits
        student_exp_ref[rows, :] = block
        tail[rows, :] = fold(block)
    part_ref[...] = row_sums(tail[...])
    head_index = lax.axis_index("head")
    first = (head_index & 3) * LANES + (head_index >> 2) * own_unit_ref.shape[0]
    own = pl.ds(pl.multiple_of(first, 16), own_unit_ref.shape[0])
    own_unit_ref[...] = unit_ref[own, :]
    own_inv_ref[...] = row_inv_ref[own, :]


def row_kernel(has_extra, *refs):
    if has_extra:
        cols_ref, exp_ref, extra_ref, msg_ref, tail = refs
    else:
        cols_ref, exp_ref, msg_ref, tail = refs
    scale = lane_tiles(1.0 / jnp.sum(cols_ref[...], axis=0), cols_ref.shape[1])

    def step(i, carry):
        start = pl.multiple_of(i * 8, 8)
        tail[pl.ds(start, 8), :] = fold(exp_ref[pl.ds(start, 8), :] * scale)
        return carry

    lax.fori_loop(0, exp_ref.shape[0] // 8, step, 0, unroll=8)
    out = row_sums(tail[...])
    if has_extra:
        out = jnp.concatenate([out, extra_ref[...]], axis=0)
    msg_ref[...] = jnp.broadcast_to(out[None], msg_ref.shape)


def col_kernel(has_extra, rows_ref, exp_ref, *refs):
    if has_extra:
        msg_ref, extra_ref, scale_ref = refs
    else:
        msg_ref, scale_ref = refs
    total = jnp.sum(rows_ref[...], axis=0)
    if has_extra:
        extra_ref[...] = total[4:8, :]
    scale = 1.0 / total[0:4, :]
    for j in range(4):
        scale_ref[j * LANES : (j + 1) * LANES, :] = column(scale[j : j + 1, :])
    count = exp_ref.shape[1] // LANES

    def step(i, sums):
        start = pl.multiple_of(i * 8, 8)
        factor = scale_ref[pl.ds(start, 8), :]
        return tuple(
            sums[k] + exp_ref[pl.ds(start, 8), k * LANES : (k + 1) * LANES] * factor
            for k in range(count)
        )

    sums = lax.fori_loop(
        0, exp_ref.shape[0] // 8, step, (jnp.zeros((8, LANES), F32),) * count, unroll=8
    )
    msg_ref[...] = jnp.concatenate([jnp.sum(s, axis=0, keepdims=True) for s in sums], axis=0)


def last_row_kernel(cols_ref, exp_ref, logits_ref, msg_ref, scale_ref, tail, weighted):
    small = 1.0 / jnp.sum(cols_ref[...], axis=0)
    scale = lane_tiles(small, cols_ref.shape[1])
    scale_ref[...] = scale

    def step(i, carry):
        start = pl.multiple_of(i * 8, 8)
        scaled = exp_ref[pl.ds(start, 8), :] * scale
        tail[pl.ds(start, 8), :] = fold(scaled)
        weighted[pl.ds(start, 8), :] = fold(scaled * logits_ref[pl.ds(start, 8), :])
        return carry

    lax.fori_loop(0, exp_ref.shape[0] // 8, step, 0, unroll=4)
    out = jnp.concatenate([row_sums(tail[...]), row_sums(weighted[...])], axis=0)
    msg_ref[...] = jnp.broadcast_to(out[None], msg_ref.shape)


def grad_kernel(
    rows_ref, partition_ref, scale_ref, exp_ref, student_ref, flip_ref, back_ref,
    weight_ref, inv_ref, keep_ref, send_ref, pull_ref, factor, softener, logits,
):
    total = jnp.sum(rows_ref[...], axis=0)
    partition = partition_ref[...]
    scale = 1.0 / total[0:4, :]
    losses = jnp.log(partition) - scale * total[4:8, :] * (1.0 / STUDENT_TEMP)
    loss = jnp.sum(jnp.sum(losses, axis=1, keepdims=True), axis=0, keepdims=True)
    columns = exp_ref.shape[1]
    for ref in (keep_ref, send_ref):
        ref[:, :, :, columns:] = jnp.broadcast_to(loss[None, None], ref.shape[:3] + (LANES,))
    softener_rows = 1.0 / partition
    for j in range(4):
        rows = slice(j * LANES, (j + 1) * LANES)
        factor[rows, :] = column(scale[j : j + 1, :])
        softener[rows, :] = column(softener_rows[j : j + 1, :])
    width = logits.shape[1]
    batch_index = lax.axis_index("batch")
    core, x_index, z_high = batch_index & 1, batch_index >> 2, (batch_index >> 1) & 1
    wide = (LANES, width)
    for block in range(columns // width):
        cols = slice(block * width, (block + 1) * width)
        for j in range(4):
            rows = slice(j * LANES, (j + 1) * LANES)
            soft = jnp.concatenate([softener[rows, :]] * (width // LANES), axis=1)
            hard = jnp.concatenate([factor[rows, :]] * (width // LANES), axis=1)
            targets = hard * (exp_ref[rows, cols] * scale_ref[0:1, cols])
            logits[rows, :] = (
                (student_ref[rows, cols] * soft - targets) * (1.0 / STUDENT_TEMP)
            ).astype(BF16)
        pull = jnp.dot(logits[...], back_ref[cols, :], preferred_element_type=F32)
        pull = pull.reshape(pull_ref.shape)
        pull_ref[...] = pull if block == 0 else pull_ref[...] + pull
        unit = jnp.dot(flip_ref[...], logits[...], preferred_element_type=F32)
        inverse = inv_ref[:, cols]
        weight_unit = weight_ref[:, cols].astype(F32) * inverse
        inner = jnp.sum(weight_unit * unit, axis=0, keepdims=True)
        full = (inverse * (unit - weight_unit * inner)).reshape(4, 2, 2, 16, width)
        first, second = full[:, :, 0], full[:, :, 1]
        for x in range(4):
            for z in range(2):
                place = ((x - x_index) & 3, z ^ z_high)
                keep_ref[place + (slice(None), cols)] = jnp.where(
                    core == 0, first[x, z], second[x, z]
                )
                send_ref[place + (slice(None), cols)] = jnp.where(
                    core == 0, second[x, z], first[x, z]
                )


def pair_kernel(pair_ref, copies_ref):
    copies_ref[...] = jnp.broadcast_to(jnp.sum(pair_ref[...], axis=0)[None], copies_ref.shape)


def finish_kernel(blocks_ref, unit_ref, inv_ref, copies_ref):
    pull = jnp.sum(blocks_ref[...], axis=0)
    unit = unit_ref[...]
    inner = jnp.sum(unit * pull, axis=1, keepdims=True)
    rows = inv_ref[:, 0:1] * (pull - unit * inner)
    copies_ref[...] = jnp.broadcast_to(rows[None], copies_ref.shape)


def exchange(blocks, axis, groups=None):
    return lax.all_to_all(blocks, axis, 0, 0, axis_index_groups=groups)


def share(block, axis, groups, count):
    return exchange(jnp.broadcast_to(block[None], (count,) + block.shape), axis, groups)


def over_batch(block):
    pairs = [[i, i + 1] for i in range(0, 16, 2)]
    rest = [[i for i in range(16) if i % 2 == core] for core in range(2)]
    both = lax.all_gather(block, "batch", axis_index_groups=pairs)
    copies = kernel_call(pair_kernel, shape((8,) + block.shape), limit=4)(both)
    return exchange(copies, "batch", rest)


def tie(*values):
    return lax.optimization_barrier(values)


def per_device(student_patches, teacher_patches, mask_index, weight):
    view_count, masked_count = mask_index.shape
    feature_dim, columns = weight.shape
    total = view_count * masked_count
    share_rows = feature_dim // 16
    y_groups = [[4 * z + y for y in range(4)] for z in range(8)]
    z_groups = [[4 * z + y for z in range(8)] for y in range(4)]
    col_msg = shape((columns // LANES, LANES))
    row_msg = shape((32, total // LANES, LANES))
    row_msg_two = shape((32, 2 * total // LANES, LANES))
    tail = pltpu.VMEM((total, LANES), F32)

    (
        back, weight_inv, teacher_exp, cols,
        unit, inverse, flip, logits, student_exp, partition_part,
    ) = kernel_call(
        start_kernel,
        (
            shape((columns, feature_dim), BF16),
            shape((1, columns)),
            shape((total, columns)),
            col_msg,
            shape((total // 32, feature_dim)),
            shape((total // 32, LANES)),
            shape((feature_dim, total), BF16),
            shape((total, columns)),
            shape((total, columns)),
            shape((total // LANES, LANES)),
        ),
        [
            pltpu.VMEM(weight.shape, BF16),
            pltpu.VMEM(teacher_patches.shape, BF16),
            pltpu.VMEM(student_patches.shape, BF16),
            pltpu.VMEM(mask_index.shape, jnp.int32),
            pltpu.VMEM((feature_dim, columns), BF16),
            pltpu.VMEM((total, feature_dim), BF16),
            pltpu.VMEM((total, feature_dim), F32),
            tail,
            tail,
            pltpu.SemaphoreType.DMA((4,)),
        ],
        far=4,
        limit=16,
    )(
        far_off(weight), far_off(teacher_patches), far_off(student_patches),
        far_off(mask_index),
    )
    cols = over_batch(cols)
    rows = kernel_call(functools.partial(row_kernel, True), row_msg_two, [tail])(
        cols, teacher_exp, partition_part
    )
    rows = exchange(rows, "head")
    cols, partition = kernel_call(
        functools.partial(col_kernel, True), (col_msg, shape((total // LANES, LANES))), [tail]
    )(rows, teacher_exp)
    cols = over_batch(cols)
    rows = kernel_call(functools.partial(row_kernel, False), row_msg, [tail])(cols, teacher_exp)
    rows = exchange(rows, "head")
    cols = kernel_call(functools.partial(col_kernel, False), col_msg, [tail])(rows, teacher_exp)
    cols = over_batch(cols)
    rows, col_scale = kernel_call(
        last_row_kernel, (row_msg_two, shape((8, columns))), [tail, tail]
    )(cols, teacher_exp, logits)
    rows = exchange(rows, "head")

    part = shape((4, 2, share_rows, columns + LANES))
    keep, send, pull = kernel_call(
        grad_kernel,
        (part, part, shape((4, total // 4, feature_dim))),
        [tail, tail, pltpu.VMEM((total, 1024), BF16)],
        limit=16,
    )(
        rows, partition, col_scale, teacher_exp, student_exp, flip, back, weight,
        weight_inv,
    )
    parts = keep + lax.ppermute(send, "batch", [(i, i ^ 1) for i in range(16)])
    parts, pull = tie(parts, pull)
    piece = jnp.sum(exchange(pull, "head", y_groups), axis=0)

    held = parts[0]
    for step in (1, 2, 3):
        pairs = [(i, (i + 4 * step) % 16) for i in range(16)]
        held = held + lax.ppermute(parts[step], "batch", pairs)

    piece = kernel_call(finish_kernel, shape((8, total // 32, feature_dim)))(
        exchange(piece.reshape(8, total // 32, feature_dim), "head", z_groups), unit, inverse
    )
    piece = exchange(piece, "head", z_groups).reshape(total // 4, feature_dim)
    grad_weight = held[0] + lax.ppermute(held[1], "batch", [(i, i ^ 2) for i in range(16)])
    grad_rows = share(piece, "head", y_groups, 4).reshape(view_count, masked_count, feature_dim)
    loss = grad_weight[0, columns] / (total * lax.axis_size("batch"))
    return (grad_rows, grad_weight[:, :columns], loss)


def solution(mesh):
    in_specs = (P("batch", None, None), P("batch", None, None), P("batch", None), P(None, "head"))
    out_specs = (P("batch", None, None), P("batch", "head"), P())
    return jax.shard_map(
        per_device, mesh=mesh, in_specs=in_specs, out_specs=out_specs, check_vma=False
    )
```
